256 devices in a mesh: grp: 64 (over z, x_lo, y), blk: 4 (over x_hi, core).
Axes of the slice: x: 4 (x_hi: 2, x_lo: 2; x = x_hi * 2 + x_lo), y: 4, z: 8, core: 2. Of those that a mesh axis runs over, the one named last changes fastest.
Arguments:
- field_phase: float32 [6, 131072], P(None, ('grp', 'blk')), may hold values from -10 to 10
- field_mass: float32 [131072], P(('grp', 'blk')), may hold values from 0.2 to 5
- old_force: float32 [6, 16384], P(None, ('grp', 'blk')), may hold values from -6 to 6
- target_slot: int32 [101, 16384], P(None, ('grp', 'blk')), may hold values from 0 to 13311, as said below
- target_star: int32 [101, 16384], P(None, ('grp', 'blk')), may hold values from 0 to 511
Outputs:
- reg_force: float32 [6, 16384], P(None, ('grp', 'blk'))
- irr_force: float32 [6, 16384], P(None, ('grp', 'blk'))
- new_state: float32 [6, 16384], P(None, ('grp', 'blk'))
The draws below stay inside these ranges and needn't reach their ends.
Inputs may be any that keep to these rules, and one draw needn't show every extreme that they name: `target_slot`: within the 64 columns of one device all slots differ; slot // 52 is the index, grp-major over grp and blk, of the device that holds the star, so at most 52 entries of one device go to one owner, and some owners receive exactly 52 from every device.
All inputs are finite; a program needn't handle non-finite values.
Results may differ from the reference program's by a relative error of at most 0.0003.
Values sent between devices are 32-bit elements; how exact they have to be, the bound alone decides.
A program may use at most 128 MiB of HBM per device.

```python
import math
import jax
import jax.numpy as jnp
from jax import lax

STAR_DEV = 512
ACT_DEV = 64
NBR = 100
STARS = 131072
ACT = 16384
MOST = 52
HOT = 64
GROUP_STARS = 2048
CLUSTERS = 64
DEVICES = 256


def draw_field_phase(key, part):
    base = jax.random.fold_in(key, 7)
    cluster_of = jnp.arange(STARS, dtype=jnp.int32) // GROUP_STARS
    centres = jax.random.normal(jax.random.fold_in(base, 1), (3, CLUSTERS), jnp.float32)
    spread = 0.8 * jax.random.normal(jax.random.fold_in(base, 2), (3, STARS), jnp.float32)
    velocity = jax.random.normal(jax.random.fold_in(base, 3), (3, STARS), jnp.float32)
    position = jnp.take(centres, cluster_of, axis=1) + spread
    return jnp.clip(jnp.concatenate([position, velocity], axis=0), -10.0, 10.0)


def draw_target_slot(key, part):
    base = jax.random.fold_in(key, 23)
    slot_total = DEVICES * MOST
    owner_rank = jax.random.permutation(jax.random.fold_in(base, 1), DEVICES)
    slot_ids = jnp.arange(slot_total, dtype=jnp.int32)
    owner_of = slot_ids // MOST
    within = slot_ids % MOST
    is_hot = jnp.take(owner_rank, owner_of) < HOT
    allowed = is_hot | (within < MOST // 2)
    target_count = ACT_DEV * (NBR + 1)

    def one_device(device):
        device_key = jax.random.fold_in(base, 1000 + device)
        scores = jax.random.permutation(jax.random.fold_in(device_key, 1), slot_total).astype(jnp.int32)
        priority = jnp.where(is_hot, scores - 2 * slot_total, jnp.where(allowed, scores, scores + 2 * slot_total))
        chosen = jnp.argsort(priority)[:target_count].astype(jnp.int32)
        mixed = jax.random.permutation(jax.random.fold_in(device_key, 2), chosen)
        return mixed.reshape(NBR + 1, ACT_DEV)
    per_device = jax.vmap(one_device)(jnp.arange(DEVICES, dtype=jnp.int32))
    return jnp.transpose(per_device, (1, 0, 2)).reshape(NBR + 1, DEVICES * ACT_DEV).astype(jnp.int32)


def plant(values, own_key, smallest, high):
    longest = values.shape.index(max(values.shape))
    spots = []
    for shift in (0, 1):
        where = [jax.random.randint(jax.random.fold_in(own_key, axis), (), 0, length) for axis, length in enumerate(values.shape)]
        where[longest] = (where[longest] + shift) % values.shape[longest]
        spots.append(tuple(where))
    return values.at[spots[0]].set(smallest).at[spots[1]].set(high)


def shard_levels(key, shape, shards, least, largest):
    loudness, own = 1.0, jax.random.fold_in(key, 6)
    for dim, blocks in shards:
        heights = jnp.exp(jax.random.uniform(jax.random.fold_in(own, dim), (blocks,), jnp.float32, least / len(shards), largest / len(shards)))
        loudness = loudness * jnp.repeat(heights, shape[dim] // blocks).reshape([-1 if axis == dim else 1 for axis in range(len(shape))])
    return loudness


def scatter_about(key, extent, scale, reach, cuts=(), kind=jnp.bfloat16):
    values = jax.random.normal(key, extent, jnp.float32) * scale
    if len(cuts) > 0:
        values = shard_levels(key, extent, cuts, -0.22, 0.18) * values
    return jnp.clip(values, min=-reach, max=reach).astype(kind)


def setup_inputs(seed: int = 0) -> dict:
    keys = jax.random.split(jax.random.key(seed), 6)
    field_phase = draw_field_phase(jax.random.fold_in(keys[5], 71), 0)
    field_mass = jnp.clip(jnp.exp(math.log(5.0) - 3.218876 * jax.random.uniform(keys[1], (STARS,), jnp.float32) ** shard_levels(keys[1], (STARS,), ((0, 256),), -0.2, 0.2)), 0.2, 5.0)
    old_force = scatter_about(keys[2], (6, ACT), 1.0, 6.0, ((1, 256),), jnp.float32)
    target_slot = draw_target_slot(jax.random.fold_in(keys[5], 71), 0)
    target_star = plant(jax.random.randint(keys[4], (NBR + 1, ACT), 0, STAR_DEV), jax.random.fold_in(keys[4], 1), 0, STAR_DEV - 1).astype(jnp.int32)
    return {"field_phase": field_phase, "field_mass": field_mass, "old_force": old_force, "target_slot": target_slot, "target_star": target_star}


soften_sq = 0.01
step_length = 0.5

def pair_block(receivers, emitters):
    separation = emitters[0:3, None, :] - receivers[0:3, :, None]
    rel_velocity = emitters[3:6, None, :] - receivers[3:6, :, None]
    dist_sq = soften_sq + lax.optimization_barrier(jnp.sum(separation * separation, axis=0))
    inverse = lax.rsqrt(dist_sq)
    weight = emitters[6][None, :] * inverse * inverse * inverse
    radial = 3.0 * lax.optimization_barrier(jnp.sum(separation * rel_velocity, axis=0)) / dist_sq
    pull_sum = lax.optimization_barrier(jnp.sum(weight[None] * separation, axis=2))
    jerk_sum = lax.optimization_barrier(jnp.sum(weight[None] * (rel_velocity - radial[None] * separation), axis=2))
    return jnp.concatenate([pull_sum, jerk_sum], axis=0)

def pair_sum(receivers, emitters):
    row_total = receivers.shape[1]
    tile_rows = math.gcd(row_total, 256)
    tiles = receivers.reshape(6, row_total // tile_rows, tile_rows).transpose(1, 0, 2)
    emit_total = emitters.shape[1]
    emit_rows = math.gcd(emit_total, 1024)
    emit_blocks = emitters.reshape(7, emit_total // emit_rows, emit_rows).transpose(1, 0, 2)

    def single_tile(block_rows):

        def add_block(total, emit_piece):
            return (total + pair_block(block_rows, emit_piece), None)
        start = jnp.zeros((6, tile_rows), jnp.float32)
        total, unused = lax.scan(add_block, start, emit_blocks)
        return total
    result = lax.map(single_tile, tiles)
    return result.transpose(1, 0, 2).reshape(6, row_total)

def neighbour_sum(receivers, emitters):
    separation = emitters[0:3] - receivers[0:3, None, :]
    rel_velocity = emitters[3:6] - receivers[3:6, None, :]
    dist_sq = soften_sq + lax.optimization_barrier(jnp.sum(separation * separation, axis=0))
    inverse = lax.rsqrt(dist_sq)
    weight = emitters[6] * inverse * inverse * inverse
    radial = 3.0 * lax.optimization_barrier(jnp.sum(separation * rel_velocity, axis=0)) / dist_sq
    pull_sum = lax.optimization_barrier(jnp.sum(weight[None] * separation, axis=1))
    jerk_sum = lax.optimization_barrier(jnp.sum(weight[None] * (rel_velocity - radial[None] * separation), axis=1))
    return jnp.concatenate([pull_sum, jerk_sum], axis=0)

def corrector(home_state, regular, irregular, old_force):
    accel_new = regular[0:3] + irregular[0:3]
    jerk_new = regular[3:6] + irregular[3:6]
    difference = old_force[0:3] - accel_new
    snap_term = -6.0 * difference - step_length * (4.0 * old_force[3:6] + 2.0 * jerk_new)
    crackle_term = 12.0 * difference + 6.0 * step_length * (old_force[3:6] + jerk_new)
    step_square = step_length * step_length
    position = home_state[0:3] + step_square / 24.0 * snap_term + step_square / 120.0 * crackle_term
    velocity = home_state[3:6] + step_length / 6.0 * snap_term + step_length / 24.0 * crackle_term
    return jnp.concatenate([position, velocity], axis=0)

def reference(field_phase, field_mass, old_force, target_slot, target_star):
    star_table = jnp.concatenate([field_phase, field_mass[None, :]], axis=0)
    global_id = (target_slot // MOST * STAR_DEV + target_star).astype(jnp.int32)
    fetched = jnp.take(star_table, global_id.reshape(-1), axis=1).reshape(7, NBR + 1, ACT)
    own_state = fetched[0:6, 0, :]
    irregular = neighbour_sum(own_state, fetched[:, 1:, :]) / NBR
    regular = pair_sum(own_state, star_table) / STARS
    return (regular, irregular, corrector(own_state, regular, irregular, old_force))
```

```python
import functools

import jax
import jax.numpy as jnp
from jax import lax
from jax.experimental import pallas as pl
from jax.experimental.pallas import tpu as pltpu
from jax.sharding import PartitionSpec as P

MESH = pl.DeviceIdType.MESH
NT = (((1,), (1,)), ((), ()))
F32 = jnp.float32
BF16 = jnp.bfloat16

SOFTEN = 0.01
STEP = 0.5
NZ, NX, NY = 8, 4, 4
STAR_DEV = 512
ACT_DEV = 64
NBR = 100
MOST = 52
OWNERS = 256
STARS = OWNERS * STAR_DEV
PAIRS = OWNERS // 2
HALF_ROWS = 51
BLOCK_ROWS = 32
UNROLL = 4


def gather_kernel(phase_ref, mass_ref, out_ref, z_send, z_recv, a_send, a_recv, b_send, b_recv, c_send, c_recv):
    grp = lax.axis_index("grp")
    blk = lax.axis_index("blk")
    z = grp // 8
    x_lo = (grp // 4) % 2
    y = grp % 4
    x = (blk // 2) * 2 + x_lo
    core = blk % 2
    a = core * x + (1 - core) * y
    b = core * y + (1 - core) * x

    def device(cz, ca, cb, cc):
        cx = core * ca + (1 - core) * cb
        cy = core * cb + (1 - core) * ca
        return (cz * 8 + (cx % 2) * 4 + cy, (cx // 2) * 2 + cc)

    a_up, a_down = (a + 1) % 4, (a + 3) % 4
    b_up, b_down = (b + 1) % 4, (b + 3) % 4
    partners = [device((z + k) % NZ, a, b, core) for k in range(1, NZ)]
    partners += [device(z, a_up, b, core), device(z, a_down, b, core)]
    partners += [device(z, a, b_up, core), device(z, a, b_down, core)]
    partners += [device(z, a, b, 1 - core)]

    out_ref[core, b, a, z, 0:6, :] = phase_ref[...]
    out_ref[core, b, a, z, 6:7, :] = mass_ref[...]
    out_ref[core, b, a, z, 7:8, :] = jnp.ones((1, STAR_DEV), F32)

    barrier = pltpu.get_barrier_semaphore()
    for partner in partners:
        pl.semaphore_signal(barrier, inc=1, device_id=partner, device_id_type=MESH)
    pl.semaphore_wait(barrier, len(partners))

    started = []

    def send(part, send_sem, recv_sem, target):
        copy = pltpu.make_async_remote_copy(
            src_ref=part, dst_ref=part, send_sem=send_sem, recv_sem=recv_sem, device_id=target, device_id_type=MESH
        )
        copy.start()
        started.append(copy)

    def await_recv(part, send_sem, recv_sem):
        pltpu.make_async_remote_copy(
            src_ref=part, dst_ref=part, send_sem=send_sem, recv_sem=recv_sem,
            device_id=partners[-1], device_id_type=MESH,
        ).wait_recv()

    def block(bb, aa):
        return out_ref.at[core, bb, aa]

    def part(bb, aa, half):
        return out_ref.at[core, bb, aa, pl.ds(4 * half, 4)]

    for k in range(1, NZ):
        send(out_ref.at[core, b, a, z], z_send.at[k], z_recv.at[k], partners[k - 1])
    for k in range(1, NZ):
        await_recv(out_ref.at[core, b, a, (z + NZ - k) % NZ], z_send.at[k], z_recv.at[k])

    to_a_up, to_a_down = partners[7], partners[8]
    to_b_up, to_b_down = partners[9], partners[10]
    other = partners[11]

    def send_core(bb, aa, n):
        send(block(bb, aa), c_send.at[n], c_recv.at[n], other)

    def send_b(aa, n):
        send(block(b, aa), b_send.at[n, 0], b_recv.at[n, 0], to_b_up)
        send(block(b, aa), b_send.at[n, 1], b_recv.at[n, 1], to_b_down)

    def near_b(aa, n):
        await_recv(block(b_down, aa), b_send.at[n, 0], b_recv.at[n, 0])
        send(part(b_down, aa, 0), b_send.at[n, 2], b_recv.at[n, 2], to_b_up)
        send_core(b_down, aa, 4 * n + 1)
        await_recv(block(b_up, aa), b_send.at[n, 1], b_recv.at[n, 1])
        send(part(b_up, aa, 1), b_send.at[n, 3], b_recv.at[n, 3], to_b_down)
        send_core(b_up, aa, 4 * n + 2)

    def far_b(aa, n):
        far = (b + 2) % 4
        await_recv(part(far, aa, 0), b_send.at[n, 2], b_recv.at[n, 2])
        await_recv(part(far, aa, 1), b_send.at[n, 3], b_recv.at[n, 3])
        send_core(far, aa, 4 * n + 3)

    send(block(b, a), a_send.at[0], a_recv.at[0], to_a_up)
    send(block(b, a), a_send.at[1], a_recv.at[1], to_a_down)
    send_b(a, 0)
    send_core(b, a, 0)

    await_recv(block(b, a_down), a_send.at[0], a_recv.at[0])
    send(part(b, a_down, 0), a_send.at[2], a_recv.at[2], to_a_up)
    send_b(a_down, 1)
    send_core(b, a_down, 4)
    await_recv(block(b, a_up), a_send.at[1], a_recv.at[1])
    send(part(b, a_up, 1), a_send.at[3], a_recv.at[3], to_a_down)
    send_b(a_up, 2)
    send_core(b, a_up, 8)
    a_far = (a + 2) % 4
    near_b(a, 0)
    await_recv(part(b, a_far, 0), a_send.at[2], a_recv.at[2])
    await_recv(part(b, a_far, 1), a_send.at[3], a_recv.at[3])
    send_b(a_far, 3)
    send_core(b, a_far, 12)
    near_b(a_down, 1)
    far_b(a, 0)
    near_b(a_up, 2)
    far_b(a_down, 1)
    near_b(a_far, 3)
    far_b(a_up, 2)
    far_b(a_far, 3)

    oa, ob = b, a
    for n, da in enumerate((0, 3, 1, 2)):
        for m, db in enumerate((0, 3, 1, 2)):
            await_recv(out_ref.at[1 - core, (ob + db) % 4, (oa + da) % 4], c_send.at[4 * n + m], c_recv.at[4 * n + m])
    for copy in started:
        copy.wait_send()


def gather_table(phase, mass):
    return pl.pallas_call(
        gather_kernel,
        out_shape=jax.ShapeDtypeStruct((2, 4, 4, NZ, 8, STAR_DEV), F32),
        in_specs=[pl.BlockSpec(memory_space=pltpu.VMEM)] * 2,
        out_specs=pl.BlockSpec(memory_space=pltpu.VMEM),
        scratch_shapes=[
            pltpu.SemaphoreType.DMA((8,)),
            pltpu.SemaphoreType.DMA((8,)),
            pltpu.SemaphoreType.DMA((4,)),
            pltpu.SemaphoreType.DMA((4,)),
            pltpu.SemaphoreType.DMA((4, 4)),
            pltpu.SemaphoreType.DMA((4, 4)),
            pltpu.SemaphoreType.DMA((16,)),
            pltpu.SemaphoreType.DMA((16,)),
        ],
        compiler_params=pltpu.CompilerParams(
            collective_id=0, has_side_effects=True, vmem_limit_bytes=24 * 2**20
        ),
        name="gather_table",
    )(phase, mass)


def split2(v):
    high = v.astype(BF16)
    return high, (v - high.astype(F32)).astype(BF16)


def split3_rows(v):
    high = v.astype(BF16).astype(F32)
    rest = v - high
    middle = rest.astype(BF16).astype(F32)
    return jnp.concatenate([high, middle, rest - middle], axis=0).astype(BF16)


def table_place(owner):
    core = owner & 1
    x = ((owner >> 1) & 1) * 2 + ((owner >> 4) & 1)
    y = (owner >> 2) & 3
    z = owner >> 5
    ab = jnp.where(core == 1, y * 4 + x, x * 4 + y)
    return core * 128 + ab * 8 + z


def force_kernel(
    table_ref, slot_ref, star_ref, old_ref, reg_ref, irr_ref, new_ref,
    own_smem, own_vec, place_scr, code_scr, column_scr, req1, req2, fetched, terms, own_b, acc, copy_sem,
):
    lane = lax.broadcasted_iota(jnp.int32, (56, 128), 1)
    row = lax.broadcasted_iota(jnp.int32, (56, 128), 0)
    place_scr[...] = jnp.zeros_like(place_scr)
    code_scr[...] = jnp.zeros_like(code_scr)
    place_scr[0:HALF_ROWS, 0:ACT_DEV] = slot_ref[0:HALF_ROWS, :]
    place_scr[0:NBR + 1 - HALF_ROWS, ACT_DEV:128] = slot_ref[HALF_ROWS:NBR + 1, :]
    code_scr[0:HALF_ROWS, 0:ACT_DEV] = star_ref[0:HALF_ROWS, :]
    code_scr[0:NBR + 1 - HALF_ROWS, ACT_DEV:128] = star_ref[HALF_ROWS:NBR + 1, :]
    slot = place_scr[...]
    star = code_scr[...]
    owner = (slot * 20165) >> 20
    within = slot - owner * MOST
    place = table_place(owner)
    active = lane & 63
    listed = (row < NBR + 1 - HALF_ROWS) | ((row == NBR + 1 - HALF_ROWS) & (lane < ACT_DEV))
    neighbour = listed & ((row > 0) | (lane >= ACT_DEV))
    place_scr[...] = jnp.where(neighbour, place >> 1, -1)
    column_scr[...] = within + 64 * (place & 1)
    code_scr[...] = star + active * 512

    own_vec[...] = jnp.zeros_like(own_vec)
    own_vec[0:1, :] = place[0:1, :] * 512 + star[0:1, :]
    fill = pltpu.make_async_copy(own_vec, own_smem, copy_sem)
    fill.start()
    fill.wait()
    lane8 = lax.broadcasted_iota(jnp.int32, (8, 128), 1)
    own = jnp.zeros((8, 128), F32)
    for i in range(ACT_DEV):
        code = own_smem[0, i]
        shard = code >> 9
        start = pl.multiple_of(((code >> 7) & 3) * 128, 128)
        tile = table_ref[shard, :, pl.ds(start, 128)]
        turned = pltpu.roll(tile, (i + 128 - (code & 127)) & 127, 1)
        own = jnp.where(lane8 == i, turned, own)
    own_columns = jnp.transpose(own)
    for c in range(6):
        own_b[c] = jnp.broadcast_to(own_columns[0:ACT_DEV, c:c + 1], (ACT_DEV, 128))

    iota128 = lax.broadcasted_iota(jnp.int32, (128, 128), 0)
    req1[...] = jnp.zeros_like(req1)
    req2[...] = jnp.zeros_like(req2)

    def add_requests(r, carry):
        rows_a, rows_1, rows_2 = [], [], []
        for k in range(2):
            line = 2 * r + k
            place_row = place_scr[pl.ds(line, 1), :]
            column_row = column_scr[pl.ds(line, 1), :]
            code_row = code_scr[pl.ds(line, 1), :]
            first = ((code_row & 127) + 128).astype(F32)
            second = (code_row >> 7).astype(F32)
            rows_a.append(jnp.where(iota128 == place_row, 1.0, 0.0).astype(BF16))
            hit = iota128 == column_row
            rows_1.append(jnp.where(hit, first, 0.0).astype(BF16))
            rows_2.append(jnp.where(hit, second, 0.0).astype(BF16))
        onehot = jnp.concatenate(rows_a, axis=1)
        req1[...] += lax.dot_general(onehot, jnp.concatenate(rows_1, axis=1), NT, preferred_element_type=F32)
        req2[...] += lax.dot_general(onehot, jnp.concatenate(rows_2, axis=1), NT, preferred_element_type=F32)
        return carry

    lax.fori_loop(0, (HALF_ROWS + 1) // 2, add_requests, 0)

    def fetch(pair, carry):
        first = jnp.broadcast_to(req1[pl.ds(pair, 1), :], (8, 128)).astype(jnp.int32)
        second = jnp.broadcast_to(req2[pl.ds(pair, 1), :], (8, 128)).astype(jnp.int32)
        index = first & 127
        quarter = second & 3
        both = []
        for h in range(2):
            got = None
            for t in range(4):
                tile = table_ref[2 * pair + h, :, t * 128:t * 128 + 128]
                column = jnp.take_along_axis(tile, index, axis=1)
                got = column if t == 0 else jnp.where(quarter == t, column, got)
            both.append(got)
        fetched[pl.ds(pl.multiple_of(pair * 8, 8), 8), :] = jnp.where(lane8 < 64, both[0], both[1])
        return carry

    lax.fori_loop(0, PAIRS, fetch, 0, unroll=4)

    def neighbour_terms(g, carry):
        base = pl.multiple_of(g * 64, 64)
        lines = pl.ds(pl.multiple_of(g * 8, 8), 8)
        first = req1[lines, :]
        index = req2[lines, :].astype(jnp.int32) >> 2
        star_rows = [fetched[pl.ds(base + c, 8, stride=8), :] for c in range(7)]
        own_rows = [
            jnp.take_along_axis(jnp.broadcast_to(own[c:c + 1, :], (8, 128)), index, axis=1) for c in range(6)
        ]
        d = [star_rows[c] - own_rows[c] for c in range(3)]
        w = [star_rows[c] - own_rows[c] for c in range(3, 6)]
        q = SOFTEN + (d[0] * d[0] + d[1] * d[1] + d[2] * d[2])
        dw = d[0] * w[0] + d[1] * w[1] + d[2] * w[2]
        inverse = lax.rsqrt(q)
        square = inverse * inverse
        weight = jnp.where(first > 0.5, star_rows[6] * inverse * square, 0.0)
        radial = 3.0 * dw * square
        for c in range(3):
            terms[pl.ds(base + c, 8, stride=8), :] = weight * d[c]
            terms[pl.ds(base + 3 + c, 8, stride=8), :] = weight * (w[c] - radial * d[c])
        terms[pl.ds(base + 6, 8, stride=8), :] = jnp.zeros((8, 128), F32)
        terms[pl.ds(base + 7, 8, stride=8), :] = jnp.zeros((8, 128), F32)
        return carry

    lax.fori_loop(0, PAIRS // 8, neighbour_terms, 0)

    iota64 = lax.broadcasted_iota(jnp.int32, (ACT_DEV, 128), 0)

    def add_terms(p, carry):
        lefts, rights = [], []
        for k in range(2):
            pair = 2 * p + k
            t = terms[pl.ds(pl.multiple_of(pair * 8, 8), 8), :]
            high = t.astype(BF16).astype(F32)
            lefts.append(jnp.concatenate([high, t - high], axis=0).astype(BF16))
            index = req2[pl.ds(pair, 1), :].astype(jnp.int32) >> 2
            rights.append(jnp.where(iota64 == index, 1.0, 0.0).astype(BF16))
        return carry + lax.dot_general(
            jnp.concatenate(lefts, axis=1), jnp.concatenate(rights, axis=1), NT, preferred_element_type=F32
        )

    sums = lax.fori_loop(0, PAIRS // 2, add_terms, jnp.zeros((16, ACT_DEV), F32), unroll=2)
    irregular = (sums[0:6, :] + sums[8:14, :]) / NBR

    acc[...] = jnp.zeros_like(acc)

    def add_shards(g, carry):
        for u in range(UNROLL):
            shard = g * UNROLL + u
            whole = table_ref[shard]
            emit = split3_rows(whole * whole[6:7, :])
            for ib in range(ACT_DEV // BLOCK_ROWS):
                rows = slice(ib * BLOCK_ROWS, (ib + 1) * BLOCK_ROWS)
                quarters = []
                for t in range(4):
                    lanes = slice(t * 128, t * 128 + 128)
                    d = [table_ref[shard, c:c + 1, lanes] - own_b[c, rows, :] for c in range(3)]
                    w = [table_ref[shard, c:c + 1, lanes] - own_b[c, rows, :] for c in range(3, 6)]
                    q = (d[0] * d[0] + d[1] * d[1]) + (d[2] * d[2] + SOFTEN)
                    dw = d[0] * w[0] + d[1] * w[1] + d[2] * w[2]
                    inverse = lax.rsqrt(q)
                    square = inverse * inverse
                    v = square * inverse
                    u_ = dw * (v * square)
                    quarters.append(split2(v) + split2(u_))
                weights = jnp.concatenate(
                    [jnp.concatenate([part[k] for part in quarters], axis=1) for k in range(4)], axis=0
                )
                acc[ib] += lax.dot_general(weights, emit, NT, preferred_element_type=F32)
        return carry

    lax.fori_loop(0, OWNERS // UNROLL, add_shards, 0)
    v_sums, u_sums = [], []
    for ib in range(ACT_DEV // BLOCK_ROWS):
        a = acc[ib]
        v_sums.append(a[0:BLOCK_ROWS] + a[BLOCK_ROWS:2 * BLOCK_ROWS])
        u_sums.append(a[2 * BLOCK_ROWS:3 * BLOCK_ROWS] + a[3 * BLOCK_ROWS:])
    pad = jnp.zeros((128 - ACT_DEV, 24), F32)

    def to_rows(s):
        s = jnp.concatenate(s + [pad], axis=0)
        s = jnp.concatenate([s, jnp.zeros((128, 104), F32)], axis=1)
        s = jnp.transpose(s)[:, 0:ACT_DEV]
        return s[0:8] + s[8:16] + s[16:24]

    v_rows = to_rows(v_sums)
    u_rows = to_rows(u_sums)
    home = own[:, 0:ACT_DEV]
    v_terms = v_rows - home * v_rows[7:8]
    u_terms = u_rows - home * u_rows[7:8]
    accel = v_terms[0:3] / STARS
    jerk = (v_terms[3:6] - 3.0 * u_terms[0:3]) / STARS

    old = old_ref[...]
    accel_new = accel + irregular[0:3]
    jerk_new = jerk + irregular[3:6]
    difference = old[0:3] - accel_new
    snap = -6.0 * difference - STEP * (4.0 * old[3:6] + 2.0 * jerk_new)
    crackle = 12.0 * difference + 6.0 * STEP * (old[3:6] + jerk_new)
    reg_ref[0:3, :] = accel
    reg_ref[3:6, :] = jerk
    irr_ref[...] = irregular
    new_ref[0:3, :] = home[0:3] + STEP * STEP / 24.0 * snap + STEP * STEP / 120.0 * crackle
    new_ref[3:6, :] = home[3:6] + STEP / 6.0 * snap + STEP / 24.0 * crackle


def forces(table, target_slot, target_star, old_force):
    vmem = pl.BlockSpec(memory_space=pltpu.VMEM)
    out = jax.ShapeDtypeStruct((6, ACT_DEV), F32)
    return pl.pallas_call(
        force_kernel,
        out_shape=(out, out, out),
        in_specs=[vmem] * 4,
        out_specs=(vmem,) * 3,
        scratch_shapes=[
            pltpu.SMEM((8, 128), jnp.int32),
            pltpu.VMEM((8, 128), jnp.int32),
            pltpu.VMEM((56, 128), jnp.int32),
            pltpu.VMEM((56, 128), jnp.int32),
            pltpu.VMEM((56, 128), jnp.int32),
            pltpu.VMEM((PAIRS, 128), F32),
            pltpu.VMEM((PAIRS, 128), F32),
            pltpu.VMEM((PAIRS * 8, 128), F32),
            pltpu.VMEM((PAIRS * 8, 128), F32),
            pltpu.VMEM((6, ACT_DEV, 128), F32),
            pltpu.VMEM((ACT_DEV // BLOCK_ROWS, 4 * BLOCK_ROWS, 24), F32),
            pltpu.SemaphoreType.DMA,
        ],
        compiler_params=pltpu.CompilerParams(vmem_limit_bytes=32 * 2**20),
        name="forces",
    )(table, target_slot, target_star, old_force)


def per_device(field_phase, field_mass, old_force, target_slot, target_star):
    table = gather_table(field_phase, field_mass.reshape(1, STAR_DEV))
    table = table.reshape(OWNERS, 8, STAR_DEV)
    return forces(table, target_slot, target_star, old_force)


def solution(mesh):
    split = P(None, ("grp", "blk"))
    return jax.shard_map(
        per_device,
        mesh=mesh,
        in_specs=(split, P(("grp", "blk")), split, split, split),
        out_specs=(split, split, split),
        check_vma=False,
    )
```

```python
import functools

import jax
import jax.numpy as jnp
from jax import lax
from jax.experimental import pallas as pl
from jax.experimental.pallas import tpu as pltpu
from jax.sharding import PartitionSpec as P

MESH = pl.DeviceIdType.MESH
NT = (((1,), (1,)), ((), ()))
F32 = jnp.float32
BF16 = jnp.bfloat16

SOFTEN = 0.01
STEP = 0.5
NZ, NX, NY = 8, 4, 4
STAR_DEV = 512
ACT_DEV = 64
NBR = 100
MOST = 52
OWNERS = 256
STARS = OWNERS * STAR_DEV
PAIRS = OWNERS // 2
HALF_ROWS = 51
UNROLL = 8


def table_place(owner):
    core = owner & 1
    x = ((owner >> 1) & 1) * 2 + ((owner >> 4) & 1)
    y = (owner >> 2) & 3
    z = owner >> 5
    ab = jnp.where(core == 1, y * 4 + x, x * 4 + y)
    return core * 128 + ab * 8 + z


def build_requests(slot_ref, star_ref, req_ref, own_ref, place_scr, code_scr, column_scr):
    lane = lax.broadcasted_iota(jnp.int32, (56, 128), 1)
    row = lax.broadcasted_iota(jnp.int32, (56, 128), 0)
    place_scr[...] = jnp.zeros_like(place_scr)
    code_scr[...] = jnp.zeros_like(code_scr)
    place_scr[0:HALF_ROWS, 0:ACT_DEV] = slot_ref[0:HALF_ROWS, :]
    place_scr[0:NBR + 1 - HALF_ROWS, ACT_DEV:128] = slot_ref[HALF_ROWS:NBR + 1, :]
    code_scr[0:HALF_ROWS, 0:ACT_DEV] = star_ref[0:HALF_ROWS, :]
    code_scr[0:NBR + 1 - HALF_ROWS, ACT_DEV:128] = star_ref[HALF_ROWS:NBR + 1, :]
    slot = place_scr[...]
    star = code_scr[...]
    owner = (slot * 20165) >> 20
    within = slot - owner * MOST
    place = table_place(owner)
    active = lane & 63
    listed = (row < NBR + 1 - HALF_ROWS) | ((row == NBR + 1 - HALF_ROWS) & (lane < ACT_DEV))
    neighbour = listed & ((row > 0) | (lane >= ACT_DEV))
    place_scr[...] = jnp.where(neighbour, place >> 1, -1)
    column_scr[...] = within + 64 * (place & 1)
    code_scr[...] = star + active * 512
    own_ref[...] = jnp.broadcast_to(place[0:1, :] * 512 + star[0:1, :], (8, 128))

    iota128 = lax.broadcasted_iota(jnp.int32, (128, 128), 0)
    req_ref[...] = jnp.zeros_like(req_ref)

    def add_requests(r, carry):
        rows_a, rows_b = [], []
        for k in range(8):
            line = 8 * r + k
            place_row = place_scr[pl.ds(line, 1), :]
            column_row = column_scr[pl.ds(line, 1), :]
            code_row = code_scr[pl.ds(line, 1), :]
            first = ((code_row & 127) + 128).astype(F32)
            second = (code_row >> 7).astype(F32)
            rows_a.append(jnp.where(iota128 == place_row, 1.0, 0.0).astype(BF16))
            hit = iota128 == column_row
            rows_b.append(
                jnp.concatenate([jnp.where(hit, first, 0.0), jnp.where(hit, second, 0.0)], axis=0).astype(BF16)
            )
        placed = lax.dot_general(
            jnp.concatenate(rows_a, axis=1), jnp.concatenate(rows_b, axis=1), NT, preferred_element_type=F32
        )
        req_ref[0] += placed[:, 0:128]
        req_ref[1] += placed[:, 128:256]
        return carry

    lax.fori_loop(0, 7, add_requests, 0)


def gather_kernel(
    phase_hbm, mass_hbm, slot_hbm, star_hbm, out_ref, req_ref, own_ref,
    phase_ref, mass_ref, slot_ref, star_ref, place_scr, code_scr, column_scr,
    in_sem, z_send, z_recv, a_send, a_recv, b_send, b_recv, c_send, c_recv,
):
    loads = [
        pltpu.make_async_copy(source, target, in_sem.at[n])
        for n, (source, target) in enumerate(
            ((phase_hbm, phase_ref), (mass_hbm, mass_ref), (slot_hbm, slot_ref), (star_hbm, star_ref))
        )
    ]
    for load in loads:
        load.start()
    grp = lax.axis_index("grp")
    blk = lax.axis_index("blk")
    z = grp // 8
    x_lo = (grp // 4) % 2
    y = grp % 4
    x = (blk // 2) * 2 + x_lo
    core = blk % 2
    a = core * x + (1 - core) * y
    b = core * y + (1 - core) * x

    def device(cz, ca, cb, cc):
        cx = core * ca + (1 - core) * cb
        cy = core * cb + (1 - core) * ca
        return (cz * 8 + (cx % 2) * 4 + cy, (cx // 2) * 2 + cc)

    a_up, a_down = (a + 1) % 4, (a + 3) % 4
    b_up, b_down = (b + 1) % 4, (b + 3) % 4
    partners = [device((z + k) % NZ, a, b, core) for k in range(1, NZ)]
    partners += [device(z, a_up, b, core), device(z, a_down, b, core)]
    partners += [device(z, a, b_up, core), device(z, a, b_down, core)]
    partners += [device(z, a, b, 1 - core), device(z, (a + 2) % 4, b, core)]

    loads[0].wait()
    loads[1].wait()

    for t in range(4):
        lanes = slice(t * 128, t * 128 + 128)
        out_ref[core, b, a, z, t, 0:6, :] = phase_ref[:, lanes]
        out_ref[core, b, a, z, t, 6:7, :] = mass_ref[:, lanes]
        out_ref[core, b, a, z, t, 7:8, :] = jnp.ones((1, 128), F32)

    barrier = pltpu.get_barrier_semaphore()
    for partner in partners:
        pl.semaphore_signal(barrier, inc=1, device_id=partner, device_id_type=MESH)
    pl.semaphore_wait(barrier, len(partners))

    started = []

    def send(part, send_sem, recv_sem, target):
        copy = pltpu.make_async_remote_copy(
            src_ref=part, dst_ref=part, send_sem=send_sem, recv_sem=recv_sem, device_id=target, device_id_type=MESH
        )
        copy.start()
        started.append(copy)

    def await_recv(part, send_sem, recv_sem):
        pltpu.make_async_remote_copy(
            src_ref=part, dst_ref=part, send_sem=send_sem, recv_sem=recv_sem,
            device_id=partners[11], device_id_type=MESH,
        ).wait_recv()

    def block(bb, aa):
        return out_ref.at[core, bb, aa]

    def part(bb, aa, half):
        return out_ref.at[core, bb, aa, pl.ds(4 * half, 4)]

    for k in range(1, NZ):
        send(out_ref.at[core, b, a, z], z_send.at[k], z_recv.at[k], partners[k - 1])
    loads[2].wait()
    loads[3].wait()
    build_requests(slot_ref, star_ref, req_ref, own_ref, place_scr, code_scr, column_scr)
    for k in range(1, NZ):
        await_recv(out_ref.at[core, b, a, (z + NZ - k) % NZ], z_send.at[k], z_recv.at[k])

    to_a_up, to_a_down = partners[7], partners[8]
    to_b_up, to_b_down = partners[9], partners[10]
    other = partners[11]

    def send_core(bb, aa, n):
        send(block(bb, aa), c_send.at[n], c_recv.at[n], other)

    def send_b(aa, n):
        send(block(b, aa), b_send.at[n, 0], b_recv.at[n, 0], to_b_up)
        send(block(b, aa), b_send.at[n, 1], b_recv.at[n, 1], to_b_down)

    def near_b(aa, n):
        await_recv(block(b_down, aa), b_send.at[n, 0], b_recv.at[n, 0])
        send(part(b_down, aa, 0), b_send.at[n, 2], b_recv.at[n, 2], to_b_up)
        send_core(b_down, aa, 4 * n + 1)
        await_recv(block(b_up, aa), b_send.at[n, 1], b_recv.at[n, 1])
        send(part(b_up, aa, 1), b_send.at[n, 3], b_recv.at[n, 3], to_b_down)
        send_core(b_up, aa, 4 * n + 2)

    def far_b(aa, n):
        far = (b + 2) % 4
        await_recv(part(far, aa, 0), b_send.at[n, 2], b_recv.at[n, 2])
        await_recv(part(far, aa, 1), b_send.at[n, 3], b_recv.at[n, 3])
        send_core(far, aa, 4 * n + 3)

    send(block(b, a), a_send.at[0], a_recv.at[0], to_a_up)
    send(block(b, a), a_send.at[1], a_recv.at[1], to_a_down)
    send(block(b, a), a_send.at[2], a_recv.at[2], partners[12])
    send_b(a, 0)
    send_core(b, a, 0)

    await_recv(block(b, a_down), a_send.at[0], a_recv.at[0])
    send_b(a_down, 1)
    send_core(b, a_down, 4)
    await_recv(block(b, a_up), a_send.at[1], a_recv.at[1])
    send_b(a_up, 2)
    send_core(b, a_up, 8)
    a_far = (a + 2) % 4
    near_b(a, 0)
    await_recv(block(b, a_far), a_send.at[2], a_recv.at[2])
    send_b(a_far, 3)
    send_core(b, a_far, 12)
    near_b(a_down, 1)
    far_b(a, 0)
    near_b(a_up, 2)
    far_b(a_down, 1)
    near_b(a_far, 3)
    far_b(a_up, 2)
    far_b(a_far, 3)

    oa, ob = b, a
    for n, da in enumerate((0, 3, 1, 2)):
        for m, db in enumerate((0, 3, 1, 2)):
            await_recv(out_ref.at[1 - core, (ob + db) % 4, (oa + da) % 4], c_send.at[4 * n + m], c_recv.at[4 * n + m])
    for copy in started:
        copy.wait_send()


def gather_table(phase, mass, target_slot, target_star):
    hbm = pl.BlockSpec(memory_space=pltpu.HBM)
    vmem = pl.BlockSpec(memory_space=pltpu.VMEM)
    return pl.pallas_call(
        gather_kernel,
        out_shape=(
            jax.ShapeDtypeStruct((2, 4, 4, NZ, 4, 8, 128), F32),
            jax.ShapeDtypeStruct((2, PAIRS, 128), F32),
            jax.ShapeDtypeStruct((8, 128), jnp.int32),
        ),
        in_specs=[hbm] * 4,
        out_specs=(vmem,) * 3,
        scratch_shapes=[
            pltpu.VMEM((6, STAR_DEV), F32),
            pltpu.VMEM((1, STAR_DEV), F32),
            pltpu.VMEM((NBR + 1, ACT_DEV), jnp.int32),
            pltpu.VMEM((NBR + 1, ACT_DEV), jnp.int32),
            pltpu.VMEM((56, 128), jnp.int32),
            pltpu.VMEM((56, 128), jnp.int32),
            pltpu.VMEM((56, 128), jnp.int32),
            pltpu.SemaphoreType.DMA((4,)),
            pltpu.SemaphoreType.DMA((8,)),
            pltpu.SemaphoreType.DMA((8,)),
            pltpu.SemaphoreType.DMA((4,)),
            pltpu.SemaphoreType.DMA((4,)),
            pltpu.SemaphoreType.DMA((4, 4)),
            pltpu.SemaphoreType.DMA((4, 4)),
            pltpu.SemaphoreType.DMA((16,)),
            pltpu.SemaphoreType.DMA((16,)),
        ],
        compiler_params=pltpu.CompilerParams(
            collective_id=0, has_side_effects=True, vmem_limit_bytes=24 * 2**20
        ),
        name="gather_table",
    )(phase, mass, target_slot, target_star)


def split2(v):
    high = v.astype(BF16)
    return high, (v - high.astype(F32)).astype(BF16)


def split3_rows(v):
    high = v.astype(BF16).astype(F32)
    rest = v - high
    middle = rest.astype(BF16).astype(F32)
    return jnp.concatenate([high, middle, rest - middle], axis=0).astype(BF16)


def force_kernel(
    table_ref, req_ref, own_vec, old_ref, reg_ref, irr_ref, new_ref,
    own_smem, fetched, terms, moved, own_b, acc, copy_sem,
):
    fill = pltpu.make_async_copy(own_vec, own_smem, copy_sem)
    fill.start()
    fill.wait()
    lane8 = lax.broadcasted_iota(jnp.int32, (8, 128), 1)
    own = jnp.zeros((8, 128), F32)
    for i in range(ACT_DEV):
        code = own_smem[0, i]
        tile = table_ref[pl.ds(pl.multiple_of((code >> 7) * 8, 8), 8), :]
        turned = pltpu.roll(tile, (i + 128 - (code & 127)) & 127, 1)
        own = jnp.where(lane8 == i, turned, own)
    own_columns = jnp.transpose(own)
    for c in range(6):
        own_b[c] = jnp.broadcast_to(own_columns[0:ACT_DEV, c:c + 1], (ACT_DEV, 128))

    def fetch(pair, carry):
        first = jnp.broadcast_to(req_ref[0, pl.ds(pair, 1), :], (8, 128)).astype(jnp.int32)
        second = jnp.broadcast_to(req_ref[1, pl.ds(pair, 1), :], (8, 128)).astype(jnp.int32)
        index = first & 127
        quarter = second & 3
        both = []
        for h in range(2):
            got = None
            for t in range(4):
                tile = table_ref[pl.ds(pl.multiple_of(pair * 64 + h * 32 + t * 8, 8), 8), :]
                column = jnp.take_along_axis(tile, index, axis=1)
                got = column if t == 0 else jnp.where(quarter == t, column, got)
            both.append(got)
        fetched[pl.ds(pl.multiple_of(pair * 8, 8), 8), :] = jnp.where(lane8 < 64, both[0], both[1])
        return carry

    lax.fori_loop(0, PAIRS, fetch, 0, unroll=4)

    def neighbour_terms(g, carry):
        base = pl.multiple_of(g * 64, 64)
        lines = pl.ds(pl.multiple_of(g * 8, 8), 8)
        first = req_ref[0, lines, :]
        index = req_ref[1, lines, :].astype(jnp.int32) >> 2
        star_rows = [fetched[pl.ds(base + c, 8, stride=8), :] for c in range(7)]
        own_rows = [
            jnp.take_along_axis(jnp.broadcast_to(own[c:c + 1, :], (8, 128)), index, axis=1) for c in range(6)
        ]
        d = [star_rows[c] - own_rows[c] for c in range(3)]
        w = [star_rows[c] - own_rows[c] for c in range(3, 6)]
        q = SOFTEN + (d[0] * d[0] + d[1] * d[1] + d[2] * d[2])
        dw = d[0] * w[0] + d[1] * w[1] + d[2] * w[2]
        inverse = lax.rsqrt(q)
        square = inverse * inverse
        weight = jnp.where(first > 0.5, star_rows[6] * inverse * square, 0.0)
        radial = 3.0 * dw * square
        for c in range(3):
            terms[pl.ds(base + c, 8, stride=8), :] = weight * d[c]
            terms[pl.ds(base + 3 + c, 8, stride=8), :] = weight * (w[c] - radial * d[c])
        terms[pl.ds(base + 6, 8, stride=8), :] = jnp.zeros((8, 128), F32)
        terms[pl.ds(base + 7, 8, stride=8), :] = jnp.zeros((8, 128), F32)
        return carry

    lax.fori_loop(0, PAIRS // 8, neighbour_terms, 0)

    iota64 = lax.broadcasted_iota(jnp.int32, (ACT_DEV, 128), 0)

    def add_terms(p, carry):
        lefts, rights = [], []
        for k in range(8):
            pair = 8 * p + k
            t = terms[pl.ds(pl.multiple_of(pair * 8, 8), 8), :]
            high = t.astype(BF16).astype(F32)
            lefts.append(jnp.concatenate([high, t - high], axis=0).astype(BF16))
            index = req_ref[1, pl.ds(pair, 1), :].astype(jnp.int32) >> 2
            rights.append(jnp.where(iota64 == index, 1.0, 0.0).astype(BF16))
        return carry + lax.dot_general(
            jnp.concatenate(lefts, axis=1), jnp.concatenate(rights, axis=1), NT, preferred_element_type=F32
        )

    sums = lax.fori_loop(0, PAIRS // 8, add_terms, jnp.zeros((16, ACT_DEV), F32))
    irregular = (sums[0:6, :] + sums[8:14, :]) / NBR

    centre = jnp.sum(own[:, 0:ACT_DEV], axis=1, keepdims=True) * (1.0 / ACT_DEV)
    home = own - centre
    for c in range(6):
        own_b[c] = own_b[c] - jnp.broadcast_to(centre[c:c + 1, :], (ACT_DEV, 128))

    def shift(g, carry):
        base = pl.multiple_of(g * 64, 64)
        rows = [table_ref[pl.ds(base + c, 8, stride=8), :] - centre[c:c + 1, :] for c in range(6)]
        for c in range(6):
            moved[pl.ds(base + c, 8, stride=8), :] = rows[c]
        moved[pl.ds(base + 6, 8, stride=8), :] = jnp.zeros((8, 128), F32)
        moved[pl.ds(base + 7, 8, stride=8), :] = jnp.ones((8, 128), F32)
        return carry

    lax.fori_loop(0, OWNERS // 2, shift, 0, unroll=2)
    acc[...] = jnp.zeros_like(acc)

    def add_shards(g, carry):
        for u in range(UNROLL):
            shard = g * UNROLL + u
            base = pl.multiple_of(shard * 32, 32)
            tiles = [pl.multiple_of(base + 8 * t, 8) for t in range(4)]
            whole = jnp.concatenate([moved[pl.ds(tile, 8), :] for tile in tiles], axis=1)
            mass = jnp.concatenate([table_ref[pl.ds(tile + 6, 1), :] for tile in tiles], axis=1)
            emit = split3_rows(whole * mass)
            quarters = []
            for t in range(4):
                d = [moved[pl.ds(tiles[t] + c, 1), :] - own_b[c] for c in range(3)]
                w = [moved[pl.ds(tiles[t] + c, 1), :] - own_b[c] for c in range(3, 6)]
                q = (d[0] * d[0] + d[1] * d[1]) + (d[2] * d[2] + SOFTEN)
                inverse = lax.rsqrt(q)
                square = inverse * inverse
                v = square * inverse
                u_ = (d[0] * w[0] + d[1] * w[1] + d[2] * w[2]) * (v * square)
                quarters.append(split2(v) + split2(u_))
            weights = jnp.concatenate(
                [jnp.concatenate([part[k] for part in quarters], axis=1) for k in range(4)], axis=0
            )
            acc[...] += lax.dot_general(emit, weights, NT, preferred_element_type=F32)
        return carry

    lax.fori_loop(0, OWNERS // UNROLL, add_shards, 0)
    total = acc[...]
    total = total[0:8] + total[8:16] + total[16:24]
    v_rows = total[:, 0:64] + total[:, 64:128]
    u_rows = total[:, 128:192] + total[:, 192:256]
    home = home[:, 0:ACT_DEV]
    v_terms = v_rows - home * v_rows[7:8]
    u_terms = u_rows - home * u_rows[7:8]
    accel = v_terms[0:3] / STARS
    jerk = (v_terms[3:6] - 3.0 * u_terms[0:3]) / STARS

    old = old_ref[...]
    accel_new = accel + irregular[0:3]
    jerk_new = jerk + irregular[3:6]
    difference = old[0:3] - accel_new
    snap = -6.0 * difference - STEP * (4.0 * old[3:6] + 2.0 * jerk_new)
    crackle = 12.0 * difference + 6.0 * STEP * (old[3:6] + jerk_new)
    reg_ref[0:3, :] = accel
    reg_ref[3:6, :] = jerk
    irr_ref[...] = irregular
    new_ref[0:3, :] = own[0:3, 0:ACT_DEV] + STEP * STEP / 24.0 * snap + STEP * STEP / 120.0 * crackle
    new_ref[3:6, :] = own[3:6, 0:ACT_DEV] + STEP / 6.0 * snap + STEP / 24.0 * crackle


def forces(table, requests, own_codes, old_force):
    vmem = pl.BlockSpec(memory_space=pltpu.VMEM)
    out = jax.ShapeDtypeStruct((6, ACT_DEV), F32)
    return pl.pallas_call(
        force_kernel,
        out_shape=(out, out, out),
        in_specs=[vmem] * 4,
        out_specs=(vmem,) * 3,
        scratch_shapes=[
            pltpu.SMEM((8, 128), jnp.int32),
            pltpu.VMEM((PAIRS * 8, 128), F32),
            pltpu.VMEM((PAIRS * 8, 128), F32),
            pltpu.VMEM((OWNERS * 32, 128), F32),
            pltpu.VMEM((6, ACT_DEV, 128), F32),
            pltpu.VMEM((24, 256), F32),
            pltpu.SemaphoreType.DMA,
        ],
        compiler_params=pltpu.CompilerParams(vmem_limit_bytes=32 * 2**20),
        name="forces",
    )(table, requests, own_codes, old_force)


def per_device(field_phase, field_mass, old_force, target_slot, target_star):
    table, requests, own_codes = gather_table(
        field_phase, field_mass.reshape(1, STAR_DEV), target_slot, target_star
    )
    return forces(table.reshape(OWNERS * 32, 128), requests, own_codes, old_force)


def solution(mesh):
    split = P(None, ("grp", "blk"))
    return jax.shard_map(
        per_device,
        mesh=mesh,
        in_specs=(split, P(("grp", "blk")), split, split, split),
        out_specs=(split, split, split),
        check_vma=False,
    )
```

```python
import functools

import jax
import jax.numpy as jnp
from jax import lax
from jax.experimental import pallas as pl
from jax.experimental.pallas import tpu as pltpu
from jax.sharding import PartitionSpec as P

MESH = pl.DeviceIdType.MESH
NT = (((1,), (1,)), ((), ()))
F32 = jnp.float32
BF16 = jnp.bfloat16

SOFTEN = 0.01
STEP = 0.5
NZ, NX, NY = 8, 4, 4
STAR_DEV = 512
ACT_DEV = 64
NBR = 100
MOST = 52
OWNERS = 256
STARS = OWNERS * STAR_DEV
PAIRS = OWNERS // 2
UNROLL = 8
STRAIGHT = 3


def table_place(owner):
    core = owner & 1
    x = ((owner >> 1) & 1) * 2 + ((owner >> 4) & 1)
    y = (owner >> 2) & 3
    z = owner >> 5
    ab = jnp.where(core == 1, y * 4 + x, x * 4 + y)
    return core * 128 + ab * 8 + z


def build_requests(slot_ref, star_ref, req_ref, own_ref, place_scr, code_scr, column_scr):
    lane = lax.broadcasted_iota(jnp.int32, (ACT_DEV, 128), 1)
    active = lax.broadcasted_iota(jnp.int32, (ACT_DEV, 128), 0)
    place_scr[...] = jnp.zeros_like(place_scr)
    code_scr[...] = jnp.zeros_like(code_scr)
    place_scr[:, 0:NBR + 1] = slot_ref[...]
    code_scr[:, 0:NBR + 1] = star_ref[...]
    slot = place_scr[...]
    star = code_scr[...]
    owner = (slot * 20165) >> 20
    within = slot - owner * MOST
    place = table_place(owner)
    place_scr[...] = jnp.where((lane > 0) & (lane <= NBR), place >> 1, -1)
    column_scr[...] = within + 64 * (place & 1)
    code_scr[...] = star + active * 512
    own_ref[...] = place * 512 + star

    iota128 = lax.broadcasted_iota(jnp.int32, (128, 128), 0)
    req_ref[...] = jnp.zeros_like(req_ref)

    def add_requests(r, carry):
        rows_a, rows_b = [], []
        for k in range(8):
            line = 8 * r + k
            place_row = place_scr[pl.ds(line, 1), :]
            column_row = column_scr[pl.ds(line, 1), :]
            code_row = code_scr[pl.ds(line, 1), :]
            first = ((code_row & 127) + 128).astype(F32)
            second = (code_row >> 7).astype(F32)
            rows_a.append(jnp.where(iota128 == place_row, 1.0, 0.0).astype(BF16))
            hit = iota128 == column_row
            rows_b.append(
                jnp.concatenate([jnp.where(hit, first, 0.0), jnp.where(hit, second, 0.0)], axis=0).astype(BF16)
            )
        placed = lax.dot_general(
            jnp.concatenate(rows_a, axis=1), jnp.concatenate(rows_b, axis=1), NT, preferred_element_type=F32
        )
        req_ref[0] += placed[:, 0:128]
        req_ref[1] += placed[:, 128:256]
        return carry

    lax.fori_loop(0, ACT_DEV // 8, add_requests, 0)


def gather_kernel(
    phase_hbm, mass_hbm, slot_hbm, star_hbm, out_ref, req_ref, own_ref, fetched,
    phase_ref, mass_ref, slot_ref, star_ref, place_scr, code_scr, column_scr,
    in_sem, z_send, z_recv, a_send, a_recv, b_send, b_recv, c_send, c_recv,
):
    loads = [
        pltpu.make_async_copy(source, target, in_sem.at[n])
        for n, (source, target) in enumerate(
            ((phase_hbm, phase_ref), (mass_hbm, mass_ref), (slot_hbm, slot_ref), (star_hbm, star_ref))
        )
    ]
    for load in loads:
        load.start()
    grp = lax.axis_index("grp")
    blk = lax.axis_index("blk")
    z = grp // 8
    x_lo = (grp // 4) % 2
    y = grp % 4
    x = (blk // 2) * 2 + x_lo
    core = blk % 2
    a = core * x + (1 - core) * y
    b = core * y + (1 - core) * x

    def device(cz, ca, cb, cc):
        cx = core * ca + (1 - core) * cb
        cy = core * cb + (1 - core) * ca
        return (cz * 8 + (cx % 2) * 4 + cy, (cx // 2) * 2 + cc)

    a_up, a_down = (a + 1) % 4, (a + 3) % 4
    b_up, b_down = (b + 1) % 4, (b + 3) % 4
    partners = [device((z + k) % NZ, a, b, core) for k in range(1, NZ)]
    partners += [device(z, a_up, b, core), device(z, a_down, b, core)]
    partners += [device(z, a, b_up, core), device(z, a, b_down, core)]
    partners += [device(z, a, b, 1 - core), device(z, (a + 2) % 4, b, core)]
    if STRAIGHT < 4:
        partners += [device(z, a, (b + 2) % 4, core)]

    loads[0].wait()
    loads[1].wait()

    for t in range(4):
        lanes = slice(t * 128, t * 128 + 128)
        out_ref[core, b, a, z, t, 0:6, :] = phase_ref[:, lanes]
        out_ref[core, b, a, z, t, 6:7, :] = mass_ref[:, lanes]
        out_ref[core, b, a, z, t, 7:8, :] = jnp.ones((1, 128), F32)

    barrier = pltpu.get_barrier_semaphore()
    for partner in partners:
        pl.semaphore_signal(barrier, inc=1, device_id=partner, device_id_type=MESH)
    pl.semaphore_wait(barrier, len(partners))

    started = []
    late = []

    def send(part, send_sem, recv_sem, target):
        copy = pltpu.make_async_remote_copy(
            src_ref=part, dst_ref=part, send_sem=send_sem, recv_sem=recv_sem, device_id=target, device_id_type=MESH
        )
        copy.start()
        started.append(copy)

    def await_recv(part, send_sem, recv_sem):
        while late:
            fetch(*late.pop())
        pltpu.make_async_remote_copy(
            src_ref=part, dst_ref=part, send_sem=send_sem, recv_sem=recv_sem,
            device_id=partners[11], device_id_type=MESH,
        ).wait_recv()

    def block(bb, aa):
        return out_ref.at[core, bb, aa]

    def part(bb, aa, half):
        return out_ref.at[core, bb, aa, pl.ds(4 * half, 4)]

    lane8 = lax.broadcasted_iota(jnp.int32, (8, 128), 1)

    def fetch(cc, bb, aa):
        def one_pair(k, carry):
            pair = cc * 64 + (bb * 4 + aa) * 4 + k
            first = jnp.broadcast_to(req_ref[0, pl.ds(pair, 1), :], (8, 128)).astype(jnp.int32)
            second = jnp.broadcast_to(req_ref[1, pl.ds(pair, 1), :], (8, 128)).astype(jnp.int32)
            index = first & 127
            quarter = second & 3
            both = []
            for h in range(2):
                got = None
                for t in range(4):
                    column = jnp.take_along_axis(out_ref[cc, bb, aa, 2 * k + h, t], index, axis=1)
                    got = column if t == 0 else jnp.where(quarter == t, column, got)
                both.append(got)
            fetched[pl.ds(pl.multiple_of(pair * 8, 8), 8), :] = jnp.where(lane8 < 64, both[0], both[1])
            return carry

        lax.fori_loop(0, 4, one_pair, 0, unroll=True)

    for k in range(1, NZ):
        send(out_ref.at[core, b, a, z], z_send.at[k], z_recv.at[k], partners[k - 1])
    loads[2].wait()
    loads[3].wait()
    build_requests(slot_ref, star_ref, req_ref, own_ref, place_scr, code_scr, column_scr)
    for k in range(1, NZ):
        await_recv(out_ref.at[core, b, a, (z + NZ - k) % NZ], z_send.at[k], z_recv.at[k])

    to_a_up, to_a_down = partners[7], partners[8]
    to_b_up, to_b_down = partners[9], partners[10]
    other = partners[11]

    def send_core(bb, aa, n):
        send(block(bb, aa), c_send.at[n], c_recv.at[n], other)
        late.append((core, bb, aa))

    def send_b(aa, n):
        send(block(b, aa), b_send.at[n, 0], b_recv.at[n, 0], to_b_up)
        send(block(b, aa), b_send.at[n, 1], b_recv.at[n, 1], to_b_down)
        if n >= STRAIGHT:
            send(block(b, aa), b_send.at[n, 2], b_recv.at[n, 2], partners[13])

    def near_b(aa, n):
        await_recv(block(b_down, aa), b_send.at[n, 0], b_recv.at[n, 0])
        if n < STRAIGHT:
            send(part(b_down, aa, 0), b_send.at[n, 2], b_recv.at[n, 2], to_b_up)
        send_core(b_down, aa, 4 * n + 1)
        await_recv(block(b_up, aa), b_send.at[n, 1], b_recv.at[n, 1])
        if n < STRAIGHT:
            send(part(b_up, aa, 1), b_send.at[n, 3], b_recv.at[n, 3], to_b_down)
        send_core(b_up, aa, 4 * n + 2)

    def far_b(aa, n):
        far = (b + 2) % 4
        if n < STRAIGHT:
            await_recv(part(far, aa, 0), b_send.at[n, 2], b_recv.at[n, 2])
            await_recv(part(far, aa, 1), b_send.at[n, 3], b_recv.at[n, 3])
        else:
            await_recv(block(far, aa), b_send.at[n, 2], b_recv.at[n, 2])
        send_core(far, aa, 4 * n + 3)

    send(block(b, a), a_send.at[0], a_recv.at[0], to_a_up)
    send(block(b, a), a_send.at[1], a_recv.at[1], to_a_down)
    send(block(b, a), a_send.at[2], a_recv.at[2], partners[12])
    send_b(a, 0)
    send_core(b, a, 0)

    await_recv(block(b, a_down), a_send.at[0], a_recv.at[0])
    send_b(a_down, 1)
    send_core(b, a_down, 4)
    await_recv(block(b, a_up), a_send.at[1], a_recv.at[1])
    send_b(a_up, 2)
    send_core(b, a_up, 8)
    a_far = (a + 2) % 4
    near_b(a, 0)
    await_recv(block(b, a_far), a_send.at[2], a_recv.at[2])
    send_b(a_far, 3)
    send_core(b, a_far, 12)
    near_b(a_down, 1)
    far_b(a, 0)
    near_b(a_up, 2)
    far_b(a_down, 1)
    near_b(a_far, 3)
    far_b(a_up, 2)
    far_b(a_far, 3)

    oa, ob = b, a
    for n, da in enumerate((0, 3, 1, 2)):
        for m, db in enumerate((0, 3, 1, 2)):
            bb, aa = (ob + db) % 4, (oa + da) % 4
            await_recv(out_ref.at[1 - core, bb, aa], c_send.at[4 * n + m], c_recv.at[4 * n + m])
            fetch(1 - core, bb, aa)
    for copy in started:
        copy.wait_send()


def gather_table(phase, mass, target_slot, target_star):
    hbm = pl.BlockSpec(memory_space=pltpu.HBM)
    vmem = pl.BlockSpec(memory_space=pltpu.VMEM)
    return pl.pallas_call(
        gather_kernel,
        out_shape=(
            jax.ShapeDtypeStruct((2, 4, 4, NZ, 4, 8, 128), F32),
            jax.ShapeDtypeStruct((2, PAIRS, 128), F32),
            jax.ShapeDtypeStruct((ACT_DEV, 128), jnp.int32),
            jax.ShapeDtypeStruct((PAIRS * 8, 128), F32),
        ),
        in_specs=[hbm] * 4,
        out_specs=(vmem,) * 4,
        scratch_shapes=[
            pltpu.VMEM((6, STAR_DEV), F32),
            pltpu.VMEM((1, STAR_DEV), F32),
            pltpu.VMEM((ACT_DEV, NBR + 1), jnp.int32),
            pltpu.VMEM((ACT_DEV, NBR + 1), jnp.int32),
            pltpu.VMEM((ACT_DEV, 128), jnp.int32),
            pltpu.VMEM((ACT_DEV, 128), jnp.int32),
            pltpu.VMEM((ACT_DEV, 128), jnp.int32),
            pltpu.SemaphoreType.DMA((4,)),
            pltpu.SemaphoreType.DMA((8,)),
            pltpu.SemaphoreType.DMA((8,)),
            pltpu.SemaphoreType.DMA((4,)),
            pltpu.SemaphoreType.DMA((4,)),
            pltpu.SemaphoreType.DMA((4, 4)),
            pltpu.SemaphoreType.DMA((4, 4)),
            pltpu.SemaphoreType.DMA((16,)),
            pltpu.SemaphoreType.DMA((16,)),
        ],
        compiler_params=pltpu.CompilerParams(
            collective_id=0, has_side_effects=True, vmem_limit_bytes=24 * 2**20
        ),
        name="gather_table",
    )(phase, mass, target_slot, target_star)


def split2(v):
    high = v.astype(BF16)
    return high, (v - high.astype(F32)).astype(BF16)


def split3_rows(v):
    high = v.astype(BF16).astype(F32)
    rest = v - high
    middle = rest.astype(BF16).astype(F32)
    return jnp.concatenate([high, middle, rest - middle], axis=0).astype(BF16)


def force_kernel(
    table_ref, req_ref, own_vec, fetched, old_ref, reg_ref, irr_ref, new_ref,
    own_smem, terms, moved, own_b, acc, copy_sem,
):
    fill = pltpu.make_async_copy(own_vec, own_smem, copy_sem)
    fill.start()
    fill.wait()
    lane8 = lax.broadcasted_iota(jnp.int32, (8, 128), 1)
    own = jnp.zeros((8, 128), F32)
    for i in range(ACT_DEV):
        code = own_smem[i, 0]
        tile = table_ref[pl.ds(pl.multiple_of((code >> 7) * 8, 8), 8), :]
        turned = pltpu.roll(tile, (i + 128 - (code & 127)) & 127, 1)
        own = jnp.where(lane8 == i, turned, own)
    own_columns = jnp.transpose(own)
    for c in range(6):
        own_b[c] = jnp.broadcast_to(own_columns[0:ACT_DEV, c:c + 1], (ACT_DEV, 128))

    def neighbour_terms(g, carry):
        base = pl.multiple_of(g * 64, 64)
        lines = pl.ds(pl.multiple_of(g * 8, 8), 8)
        first = req_ref[0, lines, :]
        index = req_ref[1, lines, :].astype(jnp.int32) >> 2
        star_rows = [fetched[pl.ds(base + c, 8, stride=8), :] for c in range(7)]
        own_rows = [
            jnp.take_along_axis(jnp.broadcast_to(own[c:c + 1, :], (8, 128)), index, axis=1) for c in range(6)
        ]
        d = [star_rows[c] - own_rows[c] for c in range(3)]
        w = [star_rows[c] - own_rows[c] for c in range(3, 6)]
        q = SOFTEN + (d[0] * d[0] + d[1] * d[1] + d[2] * d[2])
        dw = d[0] * w[0] + d[1] * w[1] + d[2] * w[2]
        inverse = lax.rsqrt(q)
        square = inverse * inverse
        weight = jnp.where(first > 0.5, star_rows[6] * inverse * square, 0.0)
        radial = 3.0 * dw * square
        for c in range(3):
            terms[pl.ds(base + c, 8, stride=8), :] = weight * d[c]
            terms[pl.ds(base + 3 + c, 8, stride=8), :] = weight * (w[c] - radial * d[c])
        terms[pl.ds(base + 6, 8, stride=8), :] = jnp.zeros((8, 128), F32)
        terms[pl.ds(base + 7, 8, stride=8), :] = jnp.zeros((8, 128), F32)
        return carry

    lax.fori_loop(0, PAIRS // 8, neighbour_terms, 0)

    iota64 = lax.broadcasted_iota(jnp.int32, (ACT_DEV, 128), 0)

    def add_terms(p, carry):
        lefts, rights = [], []
        for k in range(8):
            pair = 8 * p + k
            t = terms[pl.ds(pl.multiple_of(pair * 8, 8), 8), :]
            high = t.astype(BF16).astype(F32)
            lefts.append(jnp.concatenate([high, t - high], axis=0).astype(BF16))
            index = req_ref[1, pl.ds(pair, 1), :].astype(jnp.int32) >> 2
            rights.append(jnp.where(iota64 == index, 1.0, 0.0).astype(BF16))
        return carry + lax.dot_general(
            jnp.concatenate(lefts, axis=1), jnp.concatenate(rights, axis=1), NT, preferred_element_type=F32
        )

    sums = lax.fori_loop(0, PAIRS // 8, add_terms, jnp.zeros((16, ACT_DEV), F32))
    irregular = (sums[0:6, :] + sums[8:14, :]) / NBR

    centre = jnp.sum(own[:, 0:ACT_DEV], axis=1, keepdims=True) * (1.0 / ACT_DEV)
    home = own - centre
    for c in range(6):
        own_b[c] = own_b[c] - jnp.broadcast_to(centre[c:c + 1, :], (ACT_DEV, 128))

    def shift(g, carry):
        base = pl.multiple_of(g * 64, 64)
        rows = [table_ref[pl.ds(base + c, 8, stride=8), :] - centre[c:c + 1, :] for c in range(6)]
        for c in range(6):
            moved[pl.ds(base + c, 8, stride=8), :] = rows[c]
        moved[pl.ds(base + 6, 8, stride=8), :] = jnp.zeros((8, 128), F32)
        moved[pl.ds(base + 7, 8, stride=8), :] = jnp.ones((8, 128), F32)
        return carry

    lax.fori_loop(0, OWNERS // 2, shift, 0, unroll=2)
    acc[...] = jnp.zeros_like(acc)

    def add_shards(g, carry):
        for u in range(UNROLL):
            shard = g * UNROLL + u
            base = pl.multiple_of(shard * 32, 32)
            tiles = [pl.multiple_of(base + 8 * t, 8) for t in range(4)]
            whole = jnp.concatenate([moved[pl.ds(tile, 8), :] for tile in tiles], axis=1)
            mass = jnp.concatenate([table_ref[pl.ds(tile + 6, 1), :] for tile in tiles], axis=1)
            emit = split3_rows(whole * mass)
            quarters = []
            for t in range(4):
                d = [moved[pl.ds(tiles[t] + c, 1), :] - own_b[c] for c in range(3)]
                w = [moved[pl.ds(tiles[t] + c, 1), :] - own_b[c] for c in range(3, 6)]
                q = (d[0] * d[0] + d[1] * d[1]) + (d[2] * d[2] + SOFTEN)
                inverse = lax.rsqrt(q)
                square = inverse * inverse
                v = square * inverse
                u_ = (d[0] * w[0] + d[1] * w[1] + d[2] * w[2]) * (v * square)
                quarters.append(split2(v) + split2(u_))
            weights = jnp.concatenate(
                [jnp.concatenate([part[k] for part in quarters], axis=1) for k in range(4)], axis=0
            )
            acc[...] += lax.dot_general(emit, weights, NT, preferred_element_type=F32)
        return carry

    lax.fori_loop(0, OWNERS // UNROLL, add_shards, 0)
    total = acc[...]
    total = total[0:8] + total[8:16] + total[16:24]
    v_rows = total[:, 0:64] + total[:, 64:128]
    u_rows = total[:, 128:192] + total[:, 192:256]
    home = home[:, 0:ACT_DEV]
    v_terms = v_rows - home * v_rows[7:8]
    u_terms = u_rows - home * u_rows[7:8]
    accel = v_terms[0:3] / STARS
    jerk = (v_terms[3:6] - 3.0 * u_terms[0:3]) / STARS

    old = old_ref[...]
    accel_new = accel + irregular[0:3]
    jerk_new = jerk + irregular[3:6]
    difference = old[0:3] - accel_new
    snap = -6.0 * difference - STEP * (4.0 * old[3:6] + 2.0 * jerk_new)
    crackle = 12.0 * difference + 6.0 * STEP * (old[3:6] + jerk_new)
    reg_ref[0:3, :] = accel
    reg_ref[3:6, :] = jerk
    irr_ref[...] = irregular
    new_ref[0:3, :] = own[0:3, 0:ACT_DEV] + STEP * STEP / 24.0 * snap + STEP * STEP / 120.0 * crackle
    new_ref[3:6, :] = own[3:6, 0:ACT_DEV] + STEP / 6.0 * snap + STEP / 24.0 * crackle


def forces(table, requests, own_codes, fetched, old_force):
    vmem = pl.BlockSpec(memory_space=pltpu.VMEM)
    out = jax.ShapeDtypeStruct((6, ACT_DEV), F32)
    return pl.pallas_call(
        force_kernel,
        out_shape=(out, out, out),
        in_specs=[vmem] * 5,
        out_specs=(vmem,) * 3,
        scratch_shapes=[
            pltpu.SMEM((ACT_DEV, 128), jnp.int32),
            pltpu.VMEM((PAIRS * 8, 128), F32),
            pltpu.VMEM((OWNERS * 32, 128), F32),
            pltpu.VMEM((6, ACT_DEV, 128), F32),
            pltpu.VMEM((24, 256), F32),
            pltpu.SemaphoreType.DMA,
        ],
        compiler_params=pltpu.CompilerParams(vmem_limit_bytes=32 * 2**20),
        name="forces",
    )(table, requests, own_codes, fetched, old_force)


def per_device(field_phase, field_mass, old_force, target_slot, target_star):
    table, requests, own_codes, fetched = gather_table(
        field_phase, field_mass.reshape(1, STAR_DEV), target_slot.T, target_star.T
    )
    return forces(table.reshape(OWNERS * 32, 128), requests, own_codes, fetched, old_force)


def solution(mesh):
    split = P(None, ("grp", "blk"))
    return jax.shard_map(
        per_device,
        mesh=mesh,
        in_specs=(split, P(("grp", "blk")), split, split, split),
        out_specs=(split, split, split),
        check_vma=False,
    )
```

```python
import functools

import jax
import jax.numpy as jnp
from jax import lax
from jax.experimental import pallas as pl
from jax.experimental.pallas import tpu as pltpu
from jax.sharding import PartitionSpec as P

MESH = pl.DeviceIdType.MESH
NT = (((1,), (1,)), ((), ()))
F32 = jnp.float32
BF16 = jnp.bfloat16

SOFTEN = 0.01
STEP = 0.5
NZ, NX, NY = 8, 4, 4
STAR_DEV = 512
ACT_DEV = 64
NBR = 100
MOST = 52
OWNERS = 256
STARS = OWNERS * STAR_DEV
PAIRS = OWNERS // 2
UNROLL = 32
ON_MATRIX = (0, 4, 8, 12, 16, 20, 24, 28)
STRAIGHT = 3


def table_place(owner):
    core = owner & 1
    x = ((owner >> 1) & 1) * 2 + ((owner >> 4) & 1)
    y = (owner >> 2) & 3
    z = owner >> 5
    ab = jnp.where(core == 1, y * 4 + x, x * 4 + y)
    return core * 128 + ab * 8 + z


def build_requests(slot_ref, star_ref, req_ref, own_ref, place_scr, code_scr, column_scr):
    lane = lax.broadcasted_iota(jnp.int32, (ACT_DEV, 128), 1)
    active = lax.broadcasted_iota(jnp.int32, (ACT_DEV, 128), 0)
    place_scr[...] = jnp.zeros_like(place_scr)
    code_scr[...] = jnp.zeros_like(code_scr)
    place_scr[:, 0:NBR + 1] = slot_ref[...]
    code_scr[:, 0:NBR + 1] = star_ref[...]
    slot = place_scr[...]
    star = code_scr[...]
    owner = (slot * 20165) >> 20
    within = slot - owner * MOST
    place = table_place(owner)
    place_scr[...] = jnp.where((lane > 0) & (lane <= NBR), place >> 1, -1)
    column_scr[...] = within + 64 * (place & 1)
    code_scr[...] = star + active * 512
    own_ref[...] = place * 512 + star

    iota128 = lax.broadcasted_iota(jnp.int32, (128, 128), 0)
    req_ref[...] = jnp.zeros_like(req_ref)

    def add_requests(r, carry):
        rows_a, rows_b = [], []
        for k in range(8):
            line = 8 * r + k
            place_row = place_scr[pl.ds(line, 1), :]
            column_row = column_scr[pl.ds(line, 1), :]
            code_row = code_scr[pl.ds(line, 1), :]
            first = ((code_row & 127) + 128).astype(F32)
            second = (code_row >> 7).astype(F32)
            rows_a.append(jnp.where(iota128 == place_row, 1.0, 0.0).astype(BF16))
            hit = iota128 == column_row
            rows_b.append(
                jnp.concatenate([jnp.where(hit, first, 0.0), jnp.where(hit, second, 0.0)], axis=0).astype(BF16)
            )
        placed = lax.dot_general(
            jnp.concatenate(rows_a, axis=1), jnp.concatenate(rows_b, axis=1), NT, preferred_element_type=F32
        )
        req_ref[0] += placed[:, 0:128]
        req_ref[1] += placed[:, 128:256]
        return carry

    lax.fori_loop(0, ACT_DEV // 8, add_requests, 0)


def gather_kernel(
    phase_hbm, mass_hbm, slot_hbm, star_hbm, out_ref, req_ref, own_ref, fetched,
    phase_ref, mass_ref, slot_ref, star_ref, place_scr, code_scr, column_scr,
    in_sem, z_send, z_recv, a_send, a_recv, b_send, b_recv, c_send, c_recv,
):
    loads = [
        pltpu.make_async_copy(source, target, in_sem.at[n])
        for n, (source, target) in enumerate(
            ((phase_hbm, phase_ref), (mass_hbm, mass_ref), (slot_hbm, slot_ref), (star_hbm, star_ref))
        )
    ]
    for load in loads:
        load.start()
    grp = lax.axis_index("grp")
    blk = lax.axis_index("blk")
    z = grp // 8
    x_lo = (grp // 4) % 2
    y = grp % 4
    x = (blk // 2) * 2 + x_lo
    core = blk % 2
    a = core * x + (1 - core) * y
    b = core * y + (1 - core) * x

    def device(cz, ca, cb, cc):
        cx = core * ca + (1 - core) * cb
        cy = core * cb + (1 - core) * ca
        return (cz * 8 + (cx % 2) * 4 + cy, (cx // 2) * 2 + cc)

    a_up, a_down = (a + 1) % 4, (a + 3) % 4
    b_up, b_down = (b + 1) % 4, (b + 3) % 4
    partners = [device((z + k) % NZ, a, b, core) for k in range(1, NZ)]
    partners += [device(z, a_up, b, core), device(z, a_down, b, core)]
    partners += [device(z, a, b_up, core), device(z, a, b_down, core)]
    partners += [device(z, a, b, 1 - core), device(z, (a + 2) % 4, b, core)]
    if STRAIGHT < 4:
        partners += [device(z, a, (b + 2) % 4, core)]

    loads[0].wait()
    loads[1].wait()

    for t in range(4):
        lanes = slice(t * 128, t * 128 + 128)
        out_ref[core, b, a, z, t, 0:6, :] = phase_ref[:, lanes]
        out_ref[core, b, a, z, t, 6:7, :] = mass_ref[:, lanes]
        out_ref[core, b, a, z, t, 7:8, :] = jnp.ones((1, 128), F32)

    barrier = pltpu.get_barrier_semaphore()
    for partner in partners:
        pl.semaphore_signal(barrier, inc=1, device_id=partner, device_id_type=MESH)
    pl.semaphore_wait(barrier, len(partners))

    started = []
    late = []

    def send(part, send_sem, recv_sem, target):
        copy = pltpu.make_async_remote_copy(
            src_ref=part, dst_ref=part, send_sem=send_sem, recv_sem=recv_sem, device_id=target, device_id_type=MESH
        )
        copy.start()
        started.append(copy)

    def await_recv(part, send_sem, recv_sem):
        while late:
            fetch(*late.pop())
        pltpu.make_async_remote_copy(
            src_ref=part, dst_ref=part, send_sem=send_sem, recv_sem=recv_sem,
            device_id=partners[11], device_id_type=MESH,
        ).wait_recv()

    def block(bb, aa):
        return out_ref.at[core, bb, aa]

    def part(bb, aa, half):
        return out_ref.at[core, bb, aa, pl.ds(4 * half, 4)]

    lane8 = lax.broadcasted_iota(jnp.int32, (8, 128), 1)

    def fetch(cc, bb, aa):
        def one_pair(k, carry):
            pair = cc * 64 + (bb * 4 + aa) * 4 + k
            first = jnp.broadcast_to(req_ref[0, pl.ds(pair, 1), :], (8, 128)).astype(jnp.int32)
            second = jnp.broadcast_to(req_ref[1, pl.ds(pair, 1), :], (8, 128)).astype(jnp.int32)
            index = first & 127
            quarter = second & 3
            both = []
            for h in range(2):
                got = None
                for t in range(4):
                    column = jnp.take_along_axis(out_ref[cc, bb, aa, 2 * k + h, t], index, axis=1)
                    got = column if t == 0 else jnp.where(quarter == t, column, got)
                both.append(got)
            fetched[pl.ds(pl.multiple_of(pair * 8, 8), 8), :] = jnp.where(lane8 < 64, both[0], both[1])
            return carry

        lax.fori_loop(0, 4, one_pair, 0, unroll=True)

    for k in range(1, NZ):
        send(out_ref.at[core, b, a, z], z_send.at[k], z_recv.at[k], partners[k - 1])
    loads[2].wait()
    loads[3].wait()
    build_requests(slot_ref, star_ref, req_ref, own_ref, place_scr, code_scr, column_scr)
    for k in range(1, NZ):
        await_recv(out_ref.at[core, b, a, (z + NZ - k) % NZ], z_send.at[k], z_recv.at[k])

    to_a_up, to_a_down = partners[7], partners[8]
    to_b_up, to_b_down = partners[9], partners[10]
    other = partners[11]

    def send_core(bb, aa, n):
        send(block(bb, aa), c_send.at[n], c_recv.at[n], other)
        late.append((core, bb, aa))

    def send_b(aa, n):
        send(block(b, aa), b_send.at[n, 0], b_recv.at[n, 0], to_b_up)
        send(block(b, aa), b_send.at[n, 1], b_recv.at[n, 1], to_b_down)
        if n >= STRAIGHT:
            send(block(b, aa), b_send.at[n, 2], b_recv.at[n, 2], partners[13])

    def near_b(aa, n):
        await_recv(block(b_down, aa), b_send.at[n, 0], b_recv.at[n, 0])
        if n < STRAIGHT:
            send(part(b_down, aa, 0), b_send.at[n, 2], b_recv.at[n, 2], to_b_up)
        send_core(b_down, aa, 4 * n + 1)
        await_recv(block(b_up, aa), b_send.at[n, 1], b_recv.at[n, 1])
        if n < STRAIGHT:
            send(part(b_up, aa, 1), b_send.at[n, 3], b_recv.at[n, 3], to_b_down)
        send_core(b_up, aa, 4 * n + 2)

    def far_b(aa, n):
        far = (b + 2) % 4
        if n < STRAIGHT:
            await_recv(part(far, aa, 0), b_send.at[n, 2], b_recv.at[n, 2])
            await_recv(part(far, aa, 1), b_send.at[n, 3], b_recv.at[n, 3])
        else:
            await_recv(block(far, aa), b_send.at[n, 2], b_recv.at[n, 2])
        send_core(far, aa, 4 * n + 3)

    send(block(b, a), a_send.at[0], a_recv.at[0], to_a_up)
    send(block(b, a), a_send.at[1], a_recv.at[1], to_a_down)
    send(block(b, a), a_send.at[2], a_recv.at[2], partners[12])
    send_b(a, 0)
    send_core(b, a, 0)

    await_recv(block(b, a_down), a_send.at[0], a_recv.at[0])
    send_b(a_down, 1)
    send_core(b, a_down, 4)
    await_recv(block(b, a_up), a_send.at[1], a_recv.at[1])
    send_b(a_up, 2)
    send_core(b, a_up, 8)
    a_far = (a + 2) % 4
    near_b(a, 0)
    await_recv(block(b, a_far), a_send.at[2], a_recv.at[2])
    send_b(a_far, 3)
    send_core(b, a_far, 12)
    near_b(a_down, 1)
    far_b(a, 0)
    near_b(a_up, 2)
    far_b(a_down, 1)
    near_b(a_far, 3)
    far_b(a_up, 2)
    far_b(a_far, 3)

    oa, ob = b, a
    for n, da in enumerate((0, 3, 1, 2)):
        for m, db in enumerate((0, 3, 1, 2)):
            bb, aa = (ob + db) % 4, (oa + da) % 4
            await_recv(out_ref.at[1 - core, bb, aa], c_send.at[4 * n + m], c_recv.at[4 * n + m])
            fetch(1 - core, bb, aa)
    for copy in started:
        copy.wait_send()


def gather_table(phase, mass, target_slot, target_star):
    hbm = pl.BlockSpec(memory_space=pltpu.HBM)
    vmem = pl.BlockSpec(memory_space=pltpu.VMEM)
    return pl.pallas_call(
        gather_kernel,
        out_shape=(
            jax.ShapeDtypeStruct((2, 4, 4, NZ, 4, 8, 128), F32),
            jax.ShapeDtypeStruct((2, PAIRS, 128), F32),
            jax.ShapeDtypeStruct((ACT_DEV, 128), jnp.int32),
            jax.ShapeDtypeStruct((PAIRS * 8, 128), F32),
        ),
        in_specs=[hbm] * 4,
        out_specs=(vmem,) * 4,
        scratch_shapes=[
            pltpu.VMEM((6, STAR_DEV), F32),
            pltpu.VMEM((1, STAR_DEV), F32),
            pltpu.VMEM((ACT_DEV, NBR + 1), jnp.int32),
            pltpu.VMEM((ACT_DEV, NBR + 1), jnp.int32),
            pltpu.VMEM((ACT_DEV, 128), jnp.int32),
            pltpu.VMEM((ACT_DEV, 128), jnp.int32),
            pltpu.VMEM((ACT_DEV, 128), jnp.int32),
            pltpu.SemaphoreType.DMA((4,)),
            pltpu.SemaphoreType.DMA((8,)),
            pltpu.SemaphoreType.DMA((8,)),
            pltpu.SemaphoreType.DMA((4,)),
            pltpu.SemaphoreType.DMA((4,)),
            pltpu.SemaphoreType.DMA((4, 4)),
            pltpu.SemaphoreType.DMA((4, 4)),
            pltpu.SemaphoreType.DMA((16,)),
            pltpu.SemaphoreType.DMA((16,)),
        ],
        compiler_params=pltpu.CompilerParams(
            collective_id=0, has_side_effects=True, vmem_limit_bytes=24 * 2**20
        ),
        name="gather_table",
    )(phase, mass, target_slot, target_star)


def split2(v):
    high = v.astype(BF16)
    return high, (v - high.astype(F32)).astype(BF16)


def split3_rows(v):
    high = v.astype(BF16).astype(F32)
    rest = v - high
    middle = rest.astype(BF16).astype(F32)
    return jnp.concatenate([high, middle, rest - middle], axis=0).astype(BF16)


def force_kernel(
    table_ref, req_ref, own_vec, fetched, old_ref, reg_ref, irr_ref, new_ref,
    own_smem, terms, moved, left_scr, own_b, acc, copy_sem,
):
    fill = pltpu.make_async_copy(own_vec, own_smem, copy_sem)
    fill.start()
    fill.wait()
    lane8 = lax.broadcasted_iota(jnp.int32, (8, 128), 1)
    own = jnp.zeros((8, 128), F32)
    for i in range(ACT_DEV):
        code = own_smem[i, 0]
        tile = table_ref[pl.ds(pl.multiple_of((code >> 7) * 8, 8), 8), :]
        turned = pltpu.roll(tile, (i + 128 - (code & 127)) & 127, 1)
        own = jnp.where(lane8 == i, turned, own)
    own_columns = jnp.transpose(own)
    for c in range(6):
        own_b[c] = jnp.broadcast_to(own_columns[0:ACT_DEV, c:c + 1], (ACT_DEV, 128))

    def neighbour_terms(g):
        base = pl.multiple_of(g * 64, 64)
        lines = pl.ds(pl.multiple_of(g * 8, 8), 8)
        first = req_ref[0, lines, :]
        index = req_ref[1, lines, :].astype(jnp.int32) >> 2
        star_rows = [fetched[pl.ds(base + c, 8, stride=8), :] for c in range(7)]
        own_rows = [
            jnp.take_along_axis(jnp.broadcast_to(own[c:c + 1, :], (8, 128)), index, axis=1) for c in range(6)
        ]
        d = [star_rows[c] - own_rows[c] for c in range(3)]
        w = [star_rows[c] - own_rows[c] for c in range(3, 6)]
        q = SOFTEN + (d[0] * d[0] + d[1] * d[1] + d[2] * d[2])
        dw = d[0] * w[0] + d[1] * w[1] + d[2] * w[2]
        inverse = lax.rsqrt(q)
        square = inverse * inverse
        weight = jnp.where(first > 0.5, star_rows[6] * inverse * square, 0.0)
        radial = 3.0 * dw * square
        for c in range(3):
            terms[pl.ds(base + c, 8, stride=8), :] = weight * d[c]
            terms[pl.ds(base + 3 + c, 8, stride=8), :] = weight * (w[c] - radial * d[c])
        terms[pl.ds(base + 6, 8, stride=8), :] = jnp.zeros((8, 128), F32)
        terms[pl.ds(base + 7, 8, stride=8), :] = jnp.zeros((8, 128), F32)

    iota64 = lax.broadcasted_iota(jnp.int32, (ACT_DEV, 128), 0)

    def add_terms(p, carry):
        lefts, rights = [], []
        for k in range(8):
            pair = 8 * p + k
            t = terms[pl.ds(pl.multiple_of(pair * 8, 8), 8), :]
            high = t.astype(BF16).astype(F32)
            lefts.append(jnp.concatenate([high, t - high], axis=0).astype(BF16))
            index = req_ref[1, pl.ds(pair, 1), :].astype(jnp.int32) >> 2
            rights.append(jnp.where(iota64 == index, 1.0, 0.0).astype(BF16))
        return carry + lax.dot_general(
            jnp.concatenate(lefts, axis=1), jnp.concatenate(rights, axis=1), NT, preferred_element_type=F32
        )

    centre = jnp.sum(own[:, 0:ACT_DEV], axis=1, keepdims=True) * (1.0 / ACT_DEV)
    home = own - centre
    for c in range(6):
        own_b[c] = own_b[c] - jnp.broadcast_to(centre[c:c + 1, :], (ACT_DEV, 128))

    def shift(g, carry):
        base = pl.multiple_of(g * 64, 64)
        rows = [table_ref[pl.ds(base + c, 8, stride=8), :] - centre[c:c + 1, :] for c in range(6)]
        for c in range(6):
            moved[pl.ds(base + c, 8, stride=8), :] = rows[c]
        moved[pl.ds(base + 6, 8, stride=8), :] = rows[0] * rows[3] + rows[1] * rows[4] + rows[2] * rows[5]
        moved[pl.ds(base + 7, 8, stride=8), :] = jnp.ones((8, 128), F32)
        return carry

    lax.fori_loop(0, OWNERS // 2, shift, 0, unroll=2)
    s_own = jnp.sum(home[0:3, :] * home[3:6, :], axis=0, keepdims=True)
    left = jnp.concatenate([-home[3:6, :], -home[0:3, :], jnp.ones((1, 128), F32), s_own], axis=0)
    left_h = left.astype(BF16).astype(F32)
    left_m = (left - left_h).astype(BF16).astype(F32)
    left_l = left - left_h - left_m
    left = jnp.concatenate([left_h, left_h, left_m, left_m, left_h, left_l, jnp.zeros((80, 128), F32)], axis=0)
    left = jnp.transpose(left)[0:ACT_DEV, 0:64]
    none = jnp.zeros((ACT_DEV, 64), F32)
    for n in range(4):
        line = jnp.concatenate([left if k == n else none for k in range(4)], axis=1)
        left_scr[n * 64:n * 64 + 64, :] = line.astype(BF16)
    blank = jnp.zeros((16, 256), BF16)

    acc[...] = jnp.zeros_like(acc)

    def add_shards(g, sums):
        for k in range(UNROLL // 16):
            neighbour_terms(g * (UNROLL // 16) + k)
            sums = add_terms(g * (UNROLL // 16) + k, sums)
        wholes, products = [], []
        for u in range(UNROLL):
            tiles = [pl.multiple_of((g * UNROLL + u) * 32 + 8 * t, 8) for t in range(4)]
            wholes.append(jnp.concatenate([moved[pl.ds(tile, 8), :] for tile in tiles], axis=1))
            products.append(None)
        for first in ON_MATRIX:
            stack = []
            for u in (first, first + 1):
                high = wholes[u].astype(BF16).astype(F32)
                rest = wholes[u] - high
                middle = rest.astype(BF16).astype(F32)
                pair = jnp.concatenate([high, middle], axis=0).astype(BF16)
                last = jnp.concatenate([rest - middle, high], axis=0).astype(BF16)
                for lanes in (slice(0, 256), slice(256, 512)):
                    stack += [pair[:, lanes], pair[:, lanes], last[:, lanes], blank]
            product = jnp.dot(left_scr[...], jnp.concatenate(stack, axis=0), preferred_element_type=F32)
            for k in range(2):
                products[first + k] = jnp.concatenate(
                    [product[128 * k:128 * k + 64], product[128 * k + 64:128 * k + 128]], axis=1
                )
        on = [first + k for first in ON_MATRIX for k in range(2)]
        for u in [u for u in range(UNROLL) if u not in on] + on:
            shard = g * UNROLL + u
            base = pl.multiple_of(shard * 32, 32)
            tiles = [pl.multiple_of(base + 8 * t, 8) for t in range(4)]
            whole = wholes[u]
            mass = jnp.concatenate([table_ref[pl.ds(tile + 6, 1), :] for tile in tiles], axis=1)
            emit = split3_rows(whole * mass)
            quarters = []
            for t in range(4):
                d = [moved[pl.ds(tiles[t] + c, 1), :] - own_b[c] for c in range(3)]
                if products[u] is None:
                    w = [moved[pl.ds(tiles[t] + c, 1), :] - own_b[c] for c in range(3, 6)]
                    dw = d[0] * w[0] + d[1] * w[1] + d[2] * w[2]
                else:
                    dw = products[u][:, t * 128:t * 128 + 128]
                q = (d[0] * d[0] + d[1] * d[1]) + (d[2] * d[2] + SOFTEN)
                inverse = lax.rsqrt(q)
                square = inverse * inverse
                v = square * inverse
                u_ = dw * (v * square)
                quarters.append(split2(v) + split2(u_))
            weights = jnp.concatenate(
                [jnp.concatenate([part[k] for part in quarters], axis=1) for k in range(4)], axis=0
            )
            acc[...] += lax.dot_general(emit, weights, NT, preferred_element_type=F32)
        return sums

    sums = lax.fori_loop(0, OWNERS // UNROLL, add_shards, jnp.zeros((16, ACT_DEV), F32))
    irregular = (sums[0:6, :] + sums[8:14, :]) / NBR
    total = acc[...]
    total = total[0:8] + total[8:16] + total[16:24]
    v_rows = total[:, 0:64] + total[:, 64:128]
    u_rows = total[:, 128:192] + total[:, 192:256]
    home = home[:, 0:ACT_DEV]
    v_terms = v_rows - home * v_rows[7:8]
    u_terms = u_rows - home * u_rows[7:8]
    accel = v_terms[0:3] / STARS
    jerk = (v_terms[3:6] - 3.0 * u_terms[0:3]) / STARS

    old = old_ref[...]
    accel_new = accel + irregular[0:3]
    jerk_new = jerk + irregular[3:6]
    difference = old[0:3] - accel_new
    snap = -6.0 * difference - STEP * (4.0 * old[3:6] + 2.0 * jerk_new)
    crackle = 12.0 * difference + 6.0 * STEP * (old[3:6] + jerk_new)
    reg_ref[0:3, :] = accel
    reg_ref[3:6, :] = jerk
    irr_ref[...] = irregular
    new_ref[0:3, :] = own[0:3, 0:ACT_DEV] + STEP * STEP / 24.0 * snap + STEP * STEP / 120.0 * crackle
    new_ref[3:6, :] = own[3:6, 0:ACT_DEV] + STEP / 6.0 * snap + STEP / 24.0 * crackle


def forces(table, requests, own_codes, fetched, old_force):
    vmem = pl.BlockSpec(memory_space=pltpu.VMEM)
    out = jax.ShapeDtypeStruct((6, ACT_DEV), F32)
    return pl.pallas_call(
        force_kernel,
        out_shape=(out, out, out),
        in_specs=[vmem] * 5,
        out_specs=(vmem,) * 3,
        scratch_shapes=[
            pltpu.SMEM((ACT_DEV, 128), jnp.int32),
            pltpu.VMEM((PAIRS * 8, 128), F32),
            pltpu.VMEM((OWNERS * 32, 128), F32),
            pltpu.VMEM((256, 256), BF16),
            pltpu.VMEM((6, ACT_DEV, 128), F32),
            pltpu.VMEM((24, 256), F32),
            pltpu.SemaphoreType.DMA,
        ],
        compiler_params=pltpu.CompilerParams(vmem_limit_bytes=32 * 2**20),
        name="forces",
    )(table, requests, own_codes, fetched, old_force)


def per_device(field_phase, field_mass, old_force, target_slot, target_star):
    table, requests, own_codes, fetched = gather_table(
        field_phase, field_mass.reshape(1, STAR_DEV), target_slot.T, target_star.T
    )
    return forces(table.reshape(OWNERS * 32, 128), requests, own_codes, fetched, old_force)


def solution(mesh):
    split = P(None, ("grp", "blk"))
    return jax.shard_map(
        per_device,
        mesh=mesh,
        in_specs=(split, P(("grp", "blk")), split, split, split),
        out_specs=(split, split, split),
        check_vma=False,
    )
```

```python
import functools

import jax
import jax.numpy as jnp
from jax import lax
from jax.experimental import pallas as pl
from jax.experimental.pallas import tpu as pltpu
from jax.sharding import PartitionSpec as P

MESH = pl.DeviceIdType.MESH
NT = (((1,), (1,)), ((), ()))
F32 = jnp.float32
BF16 = jnp.bfloat16

SOFTEN = 0.01
STEP = 0.5
NZ, NX, NY = 8, 4, 4
STAR_DEV = 512
ACT_DEV = 64
NBR = 100
MOST = 52
OWNERS = 256
STARS = OWNERS * STAR_DEV
PAIRS = OWNERS // 2
UNROLL = 32
ON_MATRIX = (0, 4, 8, 12, 16, 20, 24, 28)
STRAIGHT = 3


def table_place(owner):
    core = owner & 1
    x = ((owner >> 1) & 1) * 2 + ((owner >> 4) & 1)
    y = (owner >> 2) & 3
    z = owner >> 5
    ab = jnp.where(core == 1, y * 4 + x, x * 4 + y)
    return core * 128 + ab * 8 + z


def build_requests(slot_ref, star_ref, req_ref, own_ref, place_scr, code_scr, column_scr):
    lane = lax.broadcasted_iota(jnp.int32, (ACT_DEV, 128), 1)
    active = lax.broadcasted_iota(jnp.int32, (ACT_DEV, 128), 0)
    place_scr[...] = jnp.zeros_like(place_scr)
    code_scr[...] = jnp.zeros_like(code_scr)
    place_scr[:, 0:NBR + 1] = slot_ref[...]
    code_scr[:, 0:NBR + 1] = star_ref[...]
    slot = place_scr[...]
    star = code_scr[...]
    owner = (slot * 20165) >> 20
    within = slot - owner * MOST
    place = table_place(owner)
    place_scr[...] = jnp.where((lane > 0) & (lane <= NBR), place >> 1, -1)
    column_scr[...] = within + 64 * (place & 1)
    code_scr[...] = star + active * 512
    own_ref[...] = place * 512 + star

    iota128 = lax.broadcasted_iota(jnp.int32, (128, 128), 0)
    req_ref[...] = jnp.zeros_like(req_ref)

    def add_requests(r, carry):
        rows_a, rows_b = [], []
        for k in range(8):
            line = 8 * r + k
            place_row = place_scr[pl.ds(line, 1), :]
            column_row = column_scr[pl.ds(line, 1), :]
            code_row = code_scr[pl.ds(line, 1), :]
            first = ((code_row & 127) + 128).astype(F32)
            second = (code_row >> 7).astype(F32)
            rows_a.append(jnp.where(iota128 == place_row, 1.0, 0.0).astype(BF16))
            hit = iota128 == column_row
            rows_b.append(
                jnp.concatenate([jnp.where(hit, first, 0.0), jnp.where(hit, second, 0.0)], axis=0).astype(BF16)
            )
        placed = lax.dot_general(
            jnp.concatenate(rows_a, axis=1), jnp.concatenate(rows_b, axis=1), NT, preferred_element_type=F32
        )
        req_ref[0] += placed[:, 0:128]
        req_ref[1] += placed[:, 128:256]
        return carry

    lax.fori_loop(0, ACT_DEV // 8, add_requests, 0)


def gather_kernel(
    phase_hbm, mass_hbm, slot_hbm, star_hbm, out_ref, req_ref, own_ref, fetched,
    phase_ref, mass_ref, slot_ref, star_ref, place_scr, code_scr, column_scr,
    in_sem, z_send, z_recv, a_send, a_recv, b_send, b_recv, c_send, c_recv,
):
    loads = [
        pltpu.make_async_copy(source, target, in_sem.at[n])
        for n, (source, target) in enumerate(
            ((phase_hbm, phase_ref), (mass_hbm, mass_ref), (slot_hbm, slot_ref), (star_hbm, star_ref))
        )
    ]
    for load in loads:
        load.start()
    grp = lax.axis_index("grp")
    blk = lax.axis_index("blk")
    z = grp // 8
    x_lo = (grp // 4) % 2
    y = grp % 4
    x = (blk // 2) * 2 + x_lo
    core = blk % 2
    a = core * x + (1 - core) * y
    b = core * y + (1 - core) * x

    def device(cz, ca, cb, cc):
        cx = core * ca + (1 - core) * cb
        cy = core * cb + (1 - core) * ca
        return (cz * 8 + (cx % 2) * 4 + cy, (cx // 2) * 2 + cc)

    a_up, a_down = (a + 1) % 4, (a + 3) % 4
    b_up, b_down = (b + 1) % 4, (b + 3) % 4
    partners = [device((z + k) % NZ, a, b, core) for k in range(1, NZ)]
    partners += [device(z, a_up, b, core), device(z, a_down, b, core)]
    partners += [device(z, a, b_up, core), device(z, a, b_down, core)]
    partners += [device(z, a, b, 1 - core), device(z, (a + 2) % 4, b, core)]
    if STRAIGHT < 4:
        partners += [device(z, a, (b + 2) % 4, core)]

    loads[0].wait()
    loads[1].wait()

    for t in range(4):
        lanes = slice(t * 128, t * 128 + 128)
        out_ref[core, b, a, z, t, 0:6, :] = phase_ref[:, lanes]
        out_ref[core, b, a, z, t, 6:7, :] = mass_ref[:, lanes]
        out_ref[core, b, a, z, t, 7:8, :] = jnp.ones((1, 128), F32)

    barrier = pltpu.get_barrier_semaphore()
    for partner in partners:
        pl.semaphore_signal(barrier, inc=1, device_id=partner, device_id_type=MESH)
    pl.semaphore_wait(barrier, len(partners))

    started = []
    late = []

    def send(part, send_sem, recv_sem, target):
        copy = pltpu.make_async_remote_copy(
            src_ref=part, dst_ref=part, send_sem=send_sem, recv_sem=recv_sem, device_id=target, device_id_type=MESH
        )
        copy.start()
        started.append(copy)

    def await_recv(part, send_sem, recv_sem):
        while late:
            fetch(*late.pop())
        pltpu.make_async_remote_copy(
            src_ref=part, dst_ref=part, send_sem=send_sem, recv_sem=recv_sem,
            device_id=partners[11], device_id_type=MESH,
        ).wait_recv()

    def block(bb, aa):
        return out_ref.at[core, bb, aa, :, :, pl.ds(0, 7)]

    def part(bb, aa, half):
        return out_ref.at[core, bb, aa, pl.ds(4 * half, 4), :, pl.ds(0, 7)]

    lane8 = lax.broadcasted_iota(jnp.int32, (8, 128), 1)

    def fetch(cc, bb, aa):
        def one_pair(k, carry):
            pair = cc * 64 + (bb * 4 + aa) * 4 + k
            first = jnp.broadcast_to(req_ref[0, pl.ds(pair, 1), :], (8, 128)).astype(jnp.int32)
            second = jnp.broadcast_to(req_ref[1, pl.ds(pair, 1), :], (8, 128)).astype(jnp.int32)
            index = first & 127
            quarter = second & 3
            both = []
            for h in range(2):
                got = None
                for t in range(4):
                    column = jnp.take_along_axis(out_ref[cc, bb, aa, 2 * k + h, t], index, axis=1)
                    got = column if t == 0 else jnp.where(quarter == t, column, got)
                both.append(got)
            fetched[pl.ds(pl.multiple_of(pair * 8, 8), 8), :] = jnp.where(lane8 < 64, both[0], both[1])
            return carry

        lax.fori_loop(0, 4, one_pair, 0, unroll=True)

    for k in range(1, NZ):
        send(out_ref.at[core, b, a, z, :, pl.ds(0, 7)], z_send.at[k], z_recv.at[k], partners[k - 1])
    for k in range(1, NZ):
        await_recv(out_ref.at[core, b, a, (z + NZ - k) % NZ, :, pl.ds(0, 7)], z_send.at[k], z_recv.at[k])

    to_a_up, to_a_down = partners[7], partners[8]
    to_b_up, to_b_down = partners[9], partners[10]
    other = partners[11]

    def send_core(bb, aa, n):
        send(block(bb, aa), c_send.at[n], c_recv.at[n], other)
        late.append((core, bb, aa))

    def send_b(aa, n):
        send(block(b, aa), b_send.at[n, 0], b_recv.at[n, 0], to_b_up)
        send(block(b, aa), b_send.at[n, 1], b_recv.at[n, 1], to_b_down)
        if n >= STRAIGHT:
            send(block(b, aa), b_send.at[n, 2], b_recv.at[n, 2], partners[13])

    def near_b(aa, n):
        await_recv(block(b_down, aa), b_send.at[n, 0], b_recv.at[n, 0])
        if n < STRAIGHT:
            send(part(b_down, aa, 0), b_send.at[n, 2], b_recv.at[n, 2], to_b_up)
        send_core(b_down, aa, 4 * n + 1)
        await_recv(block(b_up, aa), b_send.at[n, 1], b_recv.at[n, 1])
        if n < STRAIGHT:
            send(part(b_up, aa, 1), b_send.at[n, 3], b_recv.at[n, 3], to_b_down)
        send_core(b_up, aa, 4 * n + 2)

    def far_b(aa, n):
        far = (b + 2) % 4
        if n < STRAIGHT:
            await_recv(part(far, aa, 0), b_send.at[n, 2], b_recv.at[n, 2])
            await_recv(part(far, aa, 1), b_send.at[n, 3], b_recv.at[n, 3])
        else:
            await_recv(block(far, aa), b_send.at[n, 2], b_recv.at[n, 2])
        send_core(far, aa, 4 * n + 3)

    send(block(b, a), a_send.at[0], a_recv.at[0], to_a_up)
    send(block(b, a), a_send.at[1], a_recv.at[1], to_a_down)
    send(block(b, a), a_send.at[2], a_recv.at[2], partners[12])
    send_b(a, 0)
    send_core(b, a, 0)
    loads[2].wait()
    loads[3].wait()
    build_requests(slot_ref, star_ref, req_ref, own_ref, place_scr, code_scr, column_scr)

    await_recv(block(b, a_down), a_send.at[0], a_recv.at[0])
    send_b(a_down, 1)
    send_core(b, a_down, 4)
    await_recv(block(b, a_up), a_send.at[1], a_recv.at[1])
    send_b(a_up, 2)
    send_core(b, a_up, 8)
    a_far = (a + 2) % 4
    near_b(a, 0)
    await_recv(block(b, a_far), a_send.at[2], a_recv.at[2])
    send_b(a_far, 3)
    send_core(b, a_far, 12)
    near_b(a_down, 1)
    far_b(a, 0)
    near_b(a_up, 2)
    far_b(a_down, 1)
    near_b(a_far, 3)
    far_b(a_up, 2)
    far_b(a_far, 3)

    oa, ob = b, a
    for n, da in enumerate((0, 3, 1, 2)):
        for m, db in enumerate((0, 3, 1, 2)):
            bb, aa = (ob + db) % 4, (oa + da) % 4
            await_recv(out_ref.at[1 - core, bb, aa, :, :, pl.ds(0, 7)], c_send.at[4 * n + m], c_recv.at[4 * n + m])
            fetch(1 - core, bb, aa)
    for copy in started:
        copy.wait_send()


def gather_table(phase, mass, target_slot, target_star):
    hbm = pl.BlockSpec(memory_space=pltpu.HBM)
    vmem = pl.BlockSpec(memory_space=pltpu.VMEM)
    return pl.pallas_call(
        gather_kernel,
        out_shape=(
            jax.ShapeDtypeStruct((2, 4, 4, NZ, 4, 8, 128), F32),
            jax.ShapeDtypeStruct((2, PAIRS, 128), F32),
            jax.ShapeDtypeStruct((ACT_DEV, 128), jnp.int32),
            jax.ShapeDtypeStruct((PAIRS * 8, 128), F32),
        ),
        in_specs=[hbm] * 4,
        out_specs=(vmem,) * 4,
        scratch_shapes=[
            pltpu.VMEM((6, STAR_DEV), F32),
            pltpu.VMEM((1, STAR_DEV), F32),
            pltpu.VMEM((ACT_DEV, NBR + 1), jnp.int32),
            pltpu.VMEM((ACT_DEV, NBR + 1), jnp.int32),
            pltpu.VMEM((ACT_DEV, 128), jnp.int32),
            pltpu.VMEM((ACT_DEV, 128), jnp.int32),
            pltpu.VMEM((ACT_DEV, 128), jnp.int32),
            pltpu.SemaphoreType.DMA((4,)),
            pltpu.SemaphoreType.DMA((8,)),
            pltpu.SemaphoreType.DMA((8,)),
            pltpu.SemaphoreType.DMA((4,)),
            pltpu.SemaphoreType.DMA((4,)),
            pltpu.SemaphoreType.DMA((4, 4)),
            pltpu.SemaphoreType.DMA((4, 4)),
            pltpu.SemaphoreType.DMA((16,)),
            pltpu.SemaphoreType.DMA((16,)),
        ],
        compiler_params=pltpu.CompilerParams(
            collective_id=0, has_side_effects=True, vmem_limit_bytes=24 * 2**20
        ),
        name="gather_table",
    )(phase, mass, target_slot, target_star)


def split2(v):
    high = v.astype(BF16)
    return high, (v - high.astype(F32)).astype(BF16)


def split3_rows(v):
    high = v.astype(BF16).astype(F32)
    rest = v - high
    middle = rest.astype(BF16).astype(F32)
    return jnp.concatenate([high, middle, rest - middle], axis=0).astype(BF16)


def force_kernel(
    table_ref, req_ref, own_vec, fetched, old_hbm, reg_ref, irr_ref, new_ref,
    own_smem, old_scr, terms, moved, left_scr, own_b, acc, copy_sem, old_sem,
):
    load = pltpu.make_async_copy(old_hbm, old_scr, old_sem)
    load.start()
    fill = pltpu.make_async_copy(own_vec, own_smem, copy_sem)
    fill.start()
    fill.wait()
    lane8 = lax.broadcasted_iota(jnp.int32, (8, 128), 1)
    own = jnp.zeros((8, 128), F32)
    for i in range(ACT_DEV):
        code = own_smem[i, 0]
        tile = table_ref[pl.ds(pl.multiple_of((code >> 7) * 8, 8), 8), :]
        turned = pltpu.roll(tile, (i + 128 - (code & 127)) & 127, 1)
        own = jnp.where(lane8 == i, turned, own)
    own_columns = jnp.transpose(own)
    for c in range(6):
        own_b[c] = jnp.broadcast_to(own_columns[0:ACT_DEV, c:c + 1], (ACT_DEV, 128))

    def neighbour_terms(g):
        base = pl.multiple_of(g * 64, 64)
        lines = pl.ds(pl.multiple_of(g * 8, 8), 8)
        first = req_ref[0, lines, :]
        index = req_ref[1, lines, :].astype(jnp.int32) >> 2
        star_rows = [fetched[pl.ds(base + c, 8, stride=8), :] for c in range(7)]
        own_rows = [
            jnp.take_along_axis(jnp.broadcast_to(own[c:c + 1, :], (8, 128)), index, axis=1) for c in range(6)
        ]
        d = [star_rows[c] - own_rows[c] for c in range(3)]
        w = [star_rows[c] - own_rows[c] for c in range(3, 6)]
        q = SOFTEN + (d[0] * d[0] + d[1] * d[1] + d[2] * d[2])
        dw = d[0] * w[0] + d[1] * w[1] + d[2] * w[2]
        inverse = lax.rsqrt(q)
        square = inverse * inverse
        weight = jnp.where(first > 0.5, star_rows[6] * inverse * square, 0.0)
        radial = 3.0 * dw * square
        for c in range(3):
            terms[pl.ds(base + c, 8, stride=8), :] = weight * d[c]
            terms[pl.ds(base + 3 + c, 8, stride=8), :] = weight * (w[c] - radial * d[c])
        terms[pl.ds(base + 6, 8, stride=8), :] = jnp.zeros((8, 128), F32)
        terms[pl.ds(base + 7, 8, stride=8), :] = jnp.zeros((8, 128), F32)

    iota64 = lax.broadcasted_iota(jnp.int32, (ACT_DEV, 128), 0)

    def add_terms(p, carry):
        lefts, rights = [], []
        for k in range(8):
            pair = 8 * p + k
            t = terms[pl.ds(pl.multiple_of(pair * 8, 8), 8), :]
            high = t.astype(BF16).astype(F32)
            lefts.append(jnp.concatenate([high, t - high], axis=0).astype(BF16))
            index = req_ref[1, pl.ds(pair, 1), :].astype(jnp.int32) >> 2
            rights.append(jnp.where(iota64 == index, 1.0, 0.0).astype(BF16))
        return carry + lax.dot_general(
            jnp.concatenate(lefts, axis=1), jnp.concatenate(rights, axis=1), NT, preferred_element_type=F32
        )

    centre = jnp.sum(own[:, 0:ACT_DEV], axis=1, keepdims=True) * (1.0 / ACT_DEV)
    home = own - centre
    for c in range(6):
        own_b[c] = own_b[c] - jnp.broadcast_to(centre[c:c + 1, :], (ACT_DEV, 128))

    def shift(g, carry):
        base = pl.multiple_of(g * 64, 64)
        rows = [table_ref[pl.ds(base + c, 8, stride=8), :] - centre[c:c + 1, :] for c in range(6)]
        for c in range(6):
            moved[pl.ds(base + c, 8, stride=8), :] = rows[c]
        moved[pl.ds(base + 6, 8, stride=8), :] = rows[0] * rows[3] + rows[1] * rows[4] + rows[2] * rows[5]
        moved[pl.ds(base + 7, 8, stride=8), :] = jnp.ones((8, 128), F32)
        return carry

    lax.fori_loop(0, OWNERS // 2, shift, 0, unroll=2)
    s_own = jnp.sum(home[0:3, :] * home[3:6, :], axis=0, keepdims=True)
    left = jnp.concatenate([-home[3:6, :], -home[0:3, :], jnp.ones((1, 128), F32), s_own], axis=0)
    left_h = left.astype(BF16).astype(F32)
    left_m = (left - left_h).astype(BF16).astype(F32)
    left_l = left - left_h - left_m
    left = jnp.concatenate([left_h, left_h, left_m, left_m, left_h, left_l, jnp.zeros((80, 128), F32)], axis=0)
    left = jnp.transpose(left)[0:ACT_DEV, 0:64]
    none = jnp.zeros((ACT_DEV, 64), F32)
    for n in range(4):
        line = jnp.concatenate([left if k == n else none for k in range(4)], axis=1)
        left_scr[n * 64:n * 64 + 64, :] = line.astype(BF16)
    blank = jnp.zeros((16, 256), BF16)

    acc[...] = jnp.zeros_like(acc)

    def add_shards(g, sums):
        for k in range(UNROLL // 16):
            neighbour_terms(g * (UNROLL // 16) + k)
            sums = add_terms(g * (UNROLL // 16) + k, sums)
        wholes, products = [], []
        for u in range(UNROLL):
            tiles = [pl.multiple_of((g * UNROLL + u) * 32 + 8 * t, 8) for t in range(4)]
            wholes.append(jnp.concatenate([moved[pl.ds(tile, 8), :] for tile in tiles], axis=1))
            products.append(None)
        for first in ON_MATRIX:
            stack = []
            for u in (first, first + 1):
                high = wholes[u].astype(BF16).astype(F32)
                rest = wholes[u] - high
                middle = rest.astype(BF16).astype(F32)
                pair = jnp.concatenate([high, middle], axis=0).astype(BF16)
                last = jnp.concatenate([rest - middle, high], axis=0).astype(BF16)
                for lanes in (slice(0, 256), slice(256, 512)):
                    stack += [pair[:, lanes], pair[:, lanes], last[:, lanes], blank]
            product = jnp.dot(left_scr[...], jnp.concatenate(stack, axis=0), preferred_element_type=F32)
            for k in range(2):
                products[first + k] = jnp.concatenate(
                    [product[128 * k:128 * k + 64], product[128 * k + 64:128 * k + 128]], axis=1
                )
        on = [first + k for first in ON_MATRIX for k in range(2)]
        for u in [u for u in range(UNROLL) if u not in on] + on:
            shard = g * UNROLL + u
            base = pl.multiple_of(shard * 32, 32)
            tiles = [pl.multiple_of(base + 8 * t, 8) for t in range(4)]
            whole = wholes[u]
            mass = jnp.concatenate([table_ref[pl.ds(tile + 6, 1), :] for tile in tiles], axis=1)
            emit = split3_rows(whole * mass)
            quarters = []
            for t in range(4):
                d = [moved[pl.ds(tiles[t] + c, 1), :] - own_b[c] for c in range(3)]
                if products[u] is None:
                    w = [moved[pl.ds(tiles[t] + c, 1), :] - own_b[c] for c in range(3, 6)]
                    dw = d[0] * w[0] + d[1] * w[1] + d[2] * w[2]
                else:
                    dw = products[u][:, t * 128:t * 128 + 128]
                q = (d[0] * d[0] + d[1] * d[1]) + (d[2] * d[2] + SOFTEN)
                inverse = lax.rsqrt(q)
                square = inverse * inverse
                v = square * inverse
                u_ = dw * (v * square)
                quarters.append(split2(v) + split2(u_))
            weights = jnp.concatenate(
                [jnp.concatenate([part[k] for part in quarters], axis=1) for k in range(4)], axis=0
            )
            acc[...] += lax.dot_general(emit, weights, NT, preferred_element_type=F32)
        return sums

    sums = lax.fori_loop(0, OWNERS // UNROLL, add_shards, jnp.zeros((16, ACT_DEV), F32))
    irregular = (sums[0:6, :] + sums[8:14, :]) / NBR
    total = acc[...]
    total = total[0:8] + total[8:16] + total[16:24]
    v_rows = total[:, 0:64] + total[:, 64:128]
    u_rows = total[:, 128:192] + total[:, 192:256]
    home = home[:, 0:ACT_DEV]
    v_terms = v_rows - home * v_rows[7:8]
    u_terms = u_rows - home * u_rows[7:8]
    accel = v_terms[0:3] / STARS
    jerk = (v_terms[3:6] - 3.0 * u_terms[0:3]) / STARS

    load.wait()
    old = old_scr[...]
    accel_new = accel + irregular[0:3]
    jerk_new = jerk + irregular[3:6]
    difference = old[0:3] - accel_new
    snap = -6.0 * difference - STEP * (4.0 * old[3:6] + 2.0 * jerk_new)
    crackle = 12.0 * difference + 6.0 * STEP * (old[3:6] + jerk_new)
    reg_ref[0:3, :] = accel
    reg_ref[3:6, :] = jerk
    irr_ref[...] = irregular
    new_ref[0:3, :] = own[0:3, 0:ACT_DEV] + STEP * STEP / 24.0 * snap + STEP * STEP / 120.0 * crackle
    new_ref[3:6, :] = own[3:6, 0:ACT_DEV] + STEP / 6.0 * snap + STEP / 24.0 * crackle


def forces(table, requests, own_codes, fetched, old_force):
    vmem = pl.BlockSpec(memory_space=pltpu.VMEM)
    out = jax.ShapeDtypeStruct((6, ACT_DEV), F32)
    return pl.pallas_call(
        force_kernel,
        out_shape=(out, out, out),
        in_specs=[vmem] * 4 + [pl.BlockSpec(memory_space=pltpu.HBM)],
        out_specs=(vmem,) * 3,
        scratch_shapes=[
            pltpu.SMEM((ACT_DEV, 128), jnp.int32),
            pltpu.VMEM((6, ACT_DEV), F32),
            pltpu.VMEM((PAIRS * 8, 128), F32),
            pltpu.VMEM((OWNERS * 32, 128), F32),
            pltpu.VMEM((256, 256), BF16),
            pltpu.VMEM((6, ACT_DEV, 128), F32),
            pltpu.VMEM((24, 256), F32),
            pltpu.SemaphoreType.DMA,
            pltpu.SemaphoreType.DMA,
        ],
        compiler_params=pltpu.CompilerParams(vmem_limit_bytes=32 * 2**20),
        name="forces",
    )(table, requests, own_codes, fetched, old_force)


def in_hbm(array):
    return pltpu.with_memory_space_constraint(array, pltpu.HBM)


def per_device(field_phase, field_mass, old_force, target_slot, target_star):
    table, requests, own_codes, fetched = gather_table(
        in_hbm(field_phase), in_hbm(field_mass.reshape(1, STAR_DEV)), in_hbm(target_slot.T), in_hbm(target_star.T)
    )
    return forces(table.reshape(OWNERS * 32, 128), requests, own_codes, fetched, in_hbm(old_force))


def solution(mesh):
    split = P(None, ("grp", "blk"))
    return jax.shard_map(
        per_device,
        mesh=mesh,
        in_specs=(split, P(("grp", "blk")), split, split, split),
        out_specs=(split, split, split),
        check_vma=False,
    )
```

```python
import functools

import jax
import jax.numpy as jnp
from jax import lax
from jax.experimental import pallas as pl
from jax.experimental.pallas import tpu as pltpu
from jax.sharding import PartitionSpec as P

MESH = pl.DeviceIdType.MESH
NT = (((1,), (1,)), ((), ()))
F32 = jnp.float32
BF16 = jnp.bfloat16

SOFTEN = 0.01
STEP = 0.5
NZ, NX, NY = 8, 4, 4
STAR_DEV = 512
ACT_DEV = 64
NBR = 100
MOST = 52
OWNERS = 256
STARS = OWNERS * STAR_DEV
PAIRS = OWNERS // 2
UNROLL = 32
ON_MATRIX = (0, 4, 8, 12, 16, 20, 24, 28)
STRAIGHT = 3


def table_place(owner):
    core = owner & 1
    x = ((owner >> 1) & 1) * 2 + ((owner >> 4) & 1)
    y = (owner >> 2) & 3
    z = owner >> 5
    ab = jnp.where(core == 1, y * 4 + x, x * 4 + y)
    return core * 128 + ab * 8 + z


def build_requests(slot_ref, star_ref, req_ref, own_ref, place_scr, code_scr, column_scr):
    lane = lax.broadcasted_iota(jnp.int32, (ACT_DEV, 128), 1)
    active = lax.broadcasted_iota(jnp.int32, (ACT_DEV, 128), 0)
    place_scr[...] = jnp.zeros_like(place_scr)
    code_scr[...] = jnp.zeros_like(code_scr)
    place_scr[:, 0:NBR + 1] = slot_ref[...]
    code_scr[:, 0:NBR + 1] = star_ref[...]
    slot = place_scr[...]
    star = code_scr[...]
    owner = (slot * 20165) >> 20
    within = slot - owner * MOST
    place = table_place(owner)
    place_scr[...] = jnp.where((lane > 0) & (lane <= NBR), place >> 1, -1)
    column_scr[...] = within + 64 * (place & 1)
    code_scr[...] = star + active * 512
    own_ref[...] = place * 512 + star

    iota128 = lax.broadcasted_iota(jnp.int32, (128, 128), 0)
    req_ref[...] = jnp.zeros_like(req_ref)

    def add_requests(r, carry):
        rows_a, rows_b = [], []
        for k in range(8):
            line = 8 * r + k
            place_row = place_scr[pl.ds(line, 1), :]
            column_row = column_scr[pl.ds(line, 1), :]
            code_row = code_scr[pl.ds(line, 1), :]
            first = ((code_row & 127) + 128).astype(F32)
            second = (code_row >> 7).astype(F32)
            rows_a.append(jnp.where(iota128 == place_row, 1.0, 0.0).astype(BF16))
            hit = iota128 == column_row
            rows_b.append(
                jnp.concatenate([jnp.where(hit, first, 0.0), jnp.where(hit, second, 0.0)], axis=0).astype(BF16)
            )
        placed = lax.dot_general(
            jnp.concatenate(rows_a, axis=1), jnp.concatenate(rows_b, axis=1), NT, preferred_element_type=F32
        )
        req_ref[0] += placed[:, 0:128]
        req_ref[1] += placed[:, 128:256]
        return carry

    lax.fori_loop(0, ACT_DEV // 8, add_requests, 0)


def gather_kernel(
    phase_hbm, mass_hbm, slot_hbm, star_hbm, out_ref, req_ref, own_ref, fetched,
    phase_ref, mass_ref, slot_ref, star_ref, place_scr, code_scr, column_scr,
    in_sem, z_send, z_recv, a_send, a_recv, b_send, b_recv, c_send, c_recv,
):
    loads = [
        pltpu.make_async_copy(source, target, in_sem.at[n])
        for n, (source, target) in enumerate(
            ((phase_hbm, phase_ref), (mass_hbm, mass_ref), (slot_hbm, slot_ref), (star_hbm, star_ref))
        )
    ]
    for load in loads:
        load.start()
    grp = lax.axis_index("grp")
    blk = lax.axis_index("blk")
    z = grp // 8
    x_lo = (grp // 4) % 2
    y = grp % 4
    x = (blk // 2) * 2 + x_lo
    core = blk % 2
    a = core * x + (1 - core) * y
    b = core * y + (1 - core) * x

    def device(cz, ca, cb, cc):
        cx = core * ca + (1 - core) * cb
        cy = core * cb + (1 - core) * ca
        return (cz * 8 + (cx % 2) * 4 + cy, (cx // 2) * 2 + cc)

    a_up, a_down = (a + 1) % 4, (a + 3) % 4
    b_up, b_down = (b + 1) % 4, (b + 3) % 4
    partners = [device((z + k) % NZ, a, b, core) for k in range(1, NZ)]
    partners += [device(z, a_up, b, core), device(z, a_down, b, core)]
    partners += [device(z, a, b_up, core), device(z, a, b_down, core)]
    partners += [device(z, a, b, 1 - core), device(z, (a + 2) % 4, b, core)]
    if STRAIGHT < 4:
        partners += [device(z, a, (b + 2) % 4, core)]

    barrier = pltpu.get_barrier_semaphore()
    for partner in partners:
        pl.semaphore_signal(barrier, inc=1, device_id=partner, device_id_type=MESH)

    loads[0].wait()
    loads[1].wait()

    for t in range(4):
        lanes = slice(t * 128, t * 128 + 128)
        out_ref[core, b, a, z, t, 0:6, :] = phase_ref[:, lanes]
        out_ref[core, b, a, z, t, 6:7, :] = mass_ref[:, lanes]
        out_ref[core, b, a, z, t, 7:8, :] = jnp.ones((1, 128), F32)

    pl.semaphore_wait(barrier, len(partners))

    started = []
    late = []

    def send(part, send_sem, recv_sem, target):
        copy = pltpu.make_async_remote_copy(
            src_ref=part, dst_ref=part, send_sem=send_sem, recv_sem=recv_sem, device_id=target, device_id_type=MESH
        )
        copy.start()
        started.append(copy)

    def await_recv(part, send_sem, recv_sem):
        while late:
            fetch(*late.pop())
        pltpu.make_async_remote_copy(
            src_ref=part, dst_ref=part, send_sem=send_sem, recv_sem=recv_sem,
            device_id=partners[11], device_id_type=MESH,
        ).wait_recv()

    def block(bb, aa):
        return out_ref.at[core, bb, aa, :, :, pl.ds(0, 7)]

    def part(bb, aa, half):
        return out_ref.at[core, bb, aa, pl.ds(4 * half, 4), :, pl.ds(0, 7)]

    lane8 = lax.broadcasted_iota(jnp.int32, (8, 128), 1)

    def fetch(cc, bb, aa):
        def one_pair(k, carry):
            pair = cc * 64 + (bb * 4 + aa) * 4 + k
            first = jnp.broadcast_to(req_ref[0, pl.ds(pair, 1), :], (8, 128)).astype(jnp.int32)
            second = jnp.broadcast_to(req_ref[1, pl.ds(pair, 1), :], (8, 128)).astype(jnp.int32)
            index = first & 127
            quarter = second & 3
            both = []
            for h in range(2):
                got = None
                for t in range(4):
                    column = jnp.take_along_axis(out_ref[cc, bb, aa, 2 * k + h, t], index, axis=1)
                    got = column if t == 0 else jnp.where(quarter == t, column, got)
                both.append(got)
            fetched[pl.ds(pl.multiple_of(pair * 8, 8), 8), :] = jnp.where(lane8 < 64, both[0], both[1])
            return carry

        lax.fori_loop(0, 4, one_pair, 0, unroll=True)

    for k in range(1, NZ):
        send(out_ref.at[core, b, a, z, :, pl.ds(0, 7)], z_send.at[k], z_recv.at[k], partners[k - 1])
    for k in range(1, NZ):
        await_recv(out_ref.at[core, b, a, (z + NZ - k) % NZ, :, pl.ds(0, 7)], z_send.at[k], z_recv.at[k])

    to_a_up, to_a_down = partners[7], partners[8]
    to_b_up, to_b_down = partners[9], partners[10]
    other = partners[11]

    def send_core(bb, aa, n):
        send(block(bb, aa), c_send.at[n], c_recv.at[n], other)
        late.append((core, bb, aa))

    def send_b(aa, n):
        send(block(b, aa), b_send.at[n, 0], b_recv.at[n, 0], to_b_up)
        send(block(b, aa), b_send.at[n, 1], b_recv.at[n, 1], to_b_down)
        if n >= STRAIGHT:
            send(block(b, aa), b_send.at[n, 2], b_recv.at[n, 2], partners[13])

    def near_b(aa, n):
        await_recv(block(b_down, aa), b_send.at[n, 0], b_recv.at[n, 0])
        if n < STRAIGHT:
            send(part(b_down, aa, 0), b_send.at[n, 2], b_recv.at[n, 2], to_b_up)
        send_core(b_down, aa, 4 * n + 1)
        await_recv(block(b_up, aa), b_send.at[n, 1], b_recv.at[n, 1])
        if n < STRAIGHT:
            send(part(b_up, aa, 1), b_send.at[n, 3], b_recv.at[n, 3], to_b_down)
        send_core(b_up, aa, 4 * n + 2)

    def far_b(aa, n):
        far = (b + 2) % 4
        if n < STRAIGHT:
            await_recv(part(far, aa, 0), b_send.at[n, 2], b_recv.at[n, 2])
            await_recv(part(far, aa, 1), b_send.at[n, 3], b_recv.at[n, 3])
        else:
            await_recv(block(far, aa), b_send.at[n, 2], b_recv.at[n, 2])
        send_core(far, aa, 4 * n + 3)

    send(block(b, a), a_send.at[0], a_recv.at[0], to_a_up)
    send(block(b, a), a_send.at[1], a_recv.at[1], to_a_down)
    send(block(b, a), a_send.at[2], a_recv.at[2], partners[12])
    send_b(a, 0)
    send_core(b, a, 0)
    loads[2].wait()
    loads[3].wait()
    build_requests(slot_ref, star_ref, req_ref, own_ref, place_scr, code_scr, column_scr)

    await_recv(block(b, a_down), a_send.at[0], a_recv.at[0])
    send_b(a_down, 1)
    await_recv(block(b, a_up), a_send.at[1], a_recv.at[1])
    send_b(a_up, 2)
    send_core(b, a_down, 4)
    send_core(b, a_up, 8)
    a_far = (a + 2) % 4
    near_b(a, 0)
    await_recv(block(b, a_far), a_send.at[2], a_recv.at[2])
    send_b(a_far, 3)
    send_core(b, a_far, 12)
    near_b(a_down, 1)
    far_b(a, 0)
    near_b(a_up, 2)
    far_b(a_down, 1)
    near_b(a_far, 3)
    far_b(a_up, 2)
    far_b(a_far, 3)

    oa, ob = b, a
    for n, da in enumerate((0, 3, 1, 2)):
        for m, db in enumerate((0, 3, 1, 2)):
            bb, aa = (ob + db) % 4, (oa + da) % 4
            await_recv(out_ref.at[1 - core, bb, aa, :, :, pl.ds(0, 7)], c_send.at[4 * n + m], c_recv.at[4 * n + m])
            fetch(1 - core, bb, aa)
    for copy in started:
        copy.wait_send()


def gather_table(phase, mass, target_slot, target_star):
    hbm = pl.BlockSpec(memory_space=pltpu.HBM)
    vmem = pl.BlockSpec(memory_space=pltpu.VMEM)
    return pl.pallas_call(
        gather_kernel,
        out_shape=(
            jax.ShapeDtypeStruct((2, 4, 4, NZ, 4, 8, 128), F32),
            jax.ShapeDtypeStruct((2, PAIRS, 128), F32),
            jax.ShapeDtypeStruct((ACT_DEV, 128), jnp.int32),
            jax.ShapeDtypeStruct((PAIRS * 8, 128), F32),
        ),
        in_specs=[hbm] * 4,
        out_specs=(vmem,) * 4,
        scratch_shapes=[
            pltpu.VMEM((6, STAR_DEV), F32),
            pltpu.VMEM((1, STAR_DEV), F32),
            pltpu.VMEM((ACT_DEV, NBR + 1), jnp.int32),
            pltpu.VMEM((ACT_DEV, NBR + 1), jnp.int32),
            pltpu.VMEM((ACT_DEV, 128), jnp.int32),
            pltpu.VMEM((ACT_DEV, 128), jnp.int32),
            pltpu.VMEM((ACT_DEV, 128), jnp.int32),
            pltpu.SemaphoreType.DMA((4,)),
            pltpu.SemaphoreType.DMA((8,)),
            pltpu.SemaphoreType.DMA((8,)),
            pltpu.SemaphoreType.DMA((4,)),
            pltpu.SemaphoreType.DMA((4,)),
            pltpu.SemaphoreType.DMA((4, 4)),
            pltpu.SemaphoreType.DMA((4, 4)),
            pltpu.SemaphoreType.DMA((16,)),
            pltpu.SemaphoreType.DMA((16,)),
        ],
        compiler_params=pltpu.CompilerParams(
            collective_id=0, has_side_effects=True, vmem_limit_bytes=24 * 2**20
        ),
        name="gather_table",
    )(phase, mass, target_slot, target_star)


def split2(v):
    high = v.astype(BF16)
    return high, (v - high.astype(F32)).astype(BF16)


def split3_rows(v):
    high = v.astype(BF16).astype(F32)
    rest = v - high
    middle = rest.astype(BF16).astype(F32)
    return jnp.concatenate([high, middle, rest - middle], axis=0).astype(BF16)


def force_kernel(
    table_ref, req_ref, own_vec, fetched, old_hbm, reg_ref, irr_ref, new_ref,
    own_smem, old_scr, terms, moved, left_scr, own_b, acc, copy_sem, old_sem,
):
    load = pltpu.make_async_copy(old_hbm, old_scr, old_sem)
    load.start()
    fill = pltpu.make_async_copy(own_vec, own_smem, copy_sem)
    fill.start()
    fill.wait()
    lane8 = lax.broadcasted_iota(jnp.int32, (8, 128), 1)
    own = jnp.zeros((8, 128), F32)
    for i in range(ACT_DEV):
        code = own_smem[i, 0]
        tile = table_ref[pl.ds(pl.multiple_of((code >> 7) * 8, 8), 8), :]
        turned = pltpu.roll(tile, (i + 128 - (code & 127)) & 127, 1)
        own = jnp.where(lane8 == i, turned, own)
    own_columns = jnp.transpose(own)
    for c in range(6):
        own_b[c] = jnp.broadcast_to(own_columns[0:ACT_DEV, c:c + 1], (ACT_DEV, 128))

    def neighbour_terms(g):
        base = pl.multiple_of(g * 64, 64)
        lines = pl.ds(pl.multiple_of(g * 8, 8), 8)
        first = req_ref[0, lines, :]
        index = req_ref[1, lines, :].astype(jnp.int32) >> 2
        star_rows = [fetched[pl.ds(base + c, 8, stride=8), :] for c in range(7)]
        own_rows = [
            jnp.take_along_axis(jnp.broadcast_to(own[c:c + 1, :], (8, 128)), index, axis=1) for c in range(6)
        ]
        d = [star_rows[c] - own_rows[c] for c in range(3)]
        w = [star_rows[c] - own_rows[c] for c in range(3, 6)]
        q = SOFTEN + (d[0] * d[0] + d[1] * d[1] + d[2] * d[2])
        dw = d[0] * w[0] + d[1] * w[1] + d[2] * w[2]
        inverse = lax.rsqrt(q)
        square = inverse * inverse
        weight = jnp.where(first > 0.5, star_rows[6] * inverse * square, 0.0)
        radial = 3.0 * dw * square
        for c in range(3):
            terms[pl.ds(base + c, 8, stride=8), :] = weight * d[c]
            terms[pl.ds(base + 3 + c, 8, stride=8), :] = weight * (w[c] - radial * d[c])
        terms[pl.ds(base + 6, 8, stride=8), :] = jnp.zeros((8, 128), F32)
        terms[pl.ds(base + 7, 8, stride=8), :] = jnp.zeros((8, 128), F32)

    iota64 = lax.broadcasted_iota(jnp.int32, (ACT_DEV, 128), 0)

    def add_terms(p, carry):
        lefts, rights = [], []
        for k in range(8):
            pair = 8 * p + k
            t = terms[pl.ds(pl.multiple_of(pair * 8, 8), 8), :]
            high = t.astype(BF16).astype(F32)
            lefts.append(jnp.concatenate([high, t - high], axis=0).astype(BF16))
            index = req_ref[1, pl.ds(pair, 1), :].astype(jnp.int32) >> 2
            rights.append(jnp.where(iota64 == index, 1.0, 0.0).astype(BF16))
        return carry + lax.dot_general(
            jnp.concatenate(lefts, axis=1), jnp.concatenate(rights, axis=1), NT, preferred_element_type=F32
        )

    centre = jnp.sum(own[:, 0:ACT_DEV], axis=1, keepdims=True) * (1.0 / ACT_DEV)
    home = own - centre
    for c in range(6):
        own_b[c] = own_b[c] - jnp.broadcast_to(centre[c:c + 1, :], (ACT_DEV, 128))

    def shift(g, carry):
        base = pl.multiple_of(g * 64, 64)
        rows = [table_ref[pl.ds(base + c, 8, stride=8), :] - centre[c:c + 1, :] for c in range(6)]
        for c in range(6):
            moved[pl.ds(base + c, 8, stride=8), :] = rows[c]
        moved[pl.ds(base + 6, 8, stride=8), :] = rows[0] * rows[3] + rows[1] * rows[4] + rows[2] * rows[5]
        moved[pl.ds(base + 7, 8, stride=8), :] = jnp.ones((8, 128), F32)
        return carry

    lax.fori_loop(0, OWNERS // 2, shift, 0, unroll=2)
    s_own = jnp.sum(home[0:3, :] * home[3:6, :], axis=0, keepdims=True)
    left = jnp.concatenate([-home[3:6, :], -home[0:3, :], jnp.ones((1, 128), F32), s_own], axis=0)
    left_h = left.astype(BF16).astype(F32)
    left_m = (left - left_h).astype(BF16).astype(F32)
    left_l = left - left_h - left_m
    left = jnp.concatenate([left_h, left_h, left_m, left_m, left_h, left_l, jnp.zeros((80, 128), F32)], axis=0)
    left = jnp.transpose(left)[0:ACT_DEV, 0:64]
    none = jnp.zeros((ACT_DEV, 64), F32)
    for n in range(4):
        line = jnp.concatenate([left if k == n else none for k in range(4)], axis=1)
        left_scr[n * 64:n * 64 + 64, :] = line.astype(BF16)
    blank = jnp.zeros((16, 256), BF16)

    acc[...] = jnp.zeros_like(acc)

    def add_shards(g, sums):
        for k in range(UNROLL // 16):
            neighbour_terms(g * (UNROLL // 16) + k)
            sums = add_terms(g * (UNROLL // 16) + k, sums)
        wholes, products = [], []
        for u in range(UNROLL):
            tiles = [pl.multiple_of((g * UNROLL + u) * 32 + 8 * t, 8) for t in range(4)]
            wholes.append(jnp.concatenate([moved[pl.ds(tile, 8), :] for tile in tiles], axis=1))
            products.append(None)
        for first in ON_MATRIX:
            stack = []
            for u in (first, first + 1):
                high = wholes[u].astype(BF16).astype(F32)
                rest = wholes[u] - high
                middle = rest.astype(BF16).astype(F32)
                pair = jnp.concatenate([high, middle], axis=0).astype(BF16)
                last = jnp.concatenate([rest - middle, high], axis=0).astype(BF16)
                for lanes in (slice(0, 256), slice(256, 512)):
                    stack += [pair[:, lanes], pair[:, lanes], last[:, lanes], blank]
            product = jnp.dot(left_scr[...], jnp.concatenate(stack, axis=0), preferred_element_type=F32)
            for k in range(2):
                products[first + k] = jnp.concatenate(
                    [product[128 * k:128 * k + 64], product[128 * k + 64:128 * k + 128]], axis=1
                )
        on = [first + k for first in ON_MATRIX for k in range(2)]
        for u in [u for u in range(UNROLL) if u not in on] + on:
            shard = g * UNROLL + u
            base = pl.multiple_of(shard * 32, 32)
            tiles = [pl.multiple_of(base + 8 * t, 8) for t in range(4)]
            whole = wholes[u]
            mass = jnp.concatenate([table_ref[pl.ds(tile + 6, 1), :] for tile in tiles], axis=1)
            emit = split3_rows(whole * mass)
            quarters = []
            for t in range(4):
                d = [moved[pl.ds(tiles[t] + c, 1), :] - own_b[c] for c in range(3)]
                if products[u] is None:
                    w = [moved[pl.ds(tiles[t] + c, 1), :] - own_b[c] for c in range(3, 6)]
                    dw = d[0] * w[0] + d[1] * w[1] + d[2] * w[2]
                else:
                    dw = products[u][:, t * 128:t * 128 + 128]
                q = (d[0] * d[0] + d[1] * d[1]) + (d[2] * d[2] + SOFTEN)
                inverse = lax.rsqrt(q)
                square = inverse * inverse
                v = square * inverse
                u_ = dw * (v * square)
                quarters.append(split2(v) + split2(u_))
            weights = jnp.concatenate(
                [jnp.concatenate([part[k] for part in quarters], axis=1) for k in range(4)], axis=0
            )
            acc[...] += lax.dot_general(emit, weights, NT, preferred_element_type=F32)
        return sums

    sums = lax.fori_loop(0, OWNERS // UNROLL, add_shards, jnp.zeros((16, ACT_DEV), F32))
    irregular = (sums[0:6, :] + sums[8:14, :]) / NBR
    total = acc[...]
    total = total[0:8] + total[8:16] + total[16:24]
    v_rows = total[:, 0:64] + total[:, 64:128]
    u_rows = total[:, 128:192] + total[:, 192:256]
    home = home[:, 0:ACT_DEV]
    v_terms = v_rows - home * v_rows[7:8]
    u_terms = u_rows - home * u_rows[7:8]
    accel = v_terms[0:3] / STARS
    jerk = (v_terms[3:6] - 3.0 * u_terms[0:3]) / STARS

    load.wait()
    old = old_scr[...]
    accel_new = accel + irregular[0:3]
    jerk_new = jerk + irregular[3:6]
    difference = old[0:3] - accel_new
    snap = -6.0 * difference - STEP * (4.0 * old[3:6] + 2.0 * jerk_new)
    crackle = 12.0 * difference + 6.0 * STEP * (old[3:6] + jerk_new)
    reg_ref[0:3, :] = accel
    reg_ref[3:6, :] = jerk
    irr_ref[...] = irregular
    new_ref[0:3, :] = own[0:3, 0:ACT_DEV] + STEP * STEP / 24.0 * snap + STEP * STEP / 120.0 * crackle
    new_ref[3:6, :] = own[3:6, 0:ACT_DEV] + STEP / 6.0 * snap + STEP / 24.0 * crackle


def forces(table, requests, own_codes, fetched, old_force):
    vmem = pl.BlockSpec(memory_space=pltpu.VMEM)
    out = jax.ShapeDtypeStruct((6, ACT_DEV), F32)
    return pl.pallas_call(
        force_kernel,
        out_shape=(out, out, out),
        in_specs=[vmem] * 4 + [pl.BlockSpec(memory_space=pltpu.HBM)],
        out_specs=(vmem,) * 3,
        scratch_shapes=[
            pltpu.SMEM((ACT_DEV, 128), jnp.int32),
            pltpu.VMEM((6, ACT_DEV), F32),
            pltpu.VMEM((PAIRS * 8, 128), F32),
            pltpu.VMEM((OWNERS * 32, 128), F32),
            pltpu.VMEM((256, 256), BF16),
            pltpu.VMEM((6, ACT_DEV, 128), F32),
            pltpu.VMEM((24, 256), F32),
            pltpu.SemaphoreType.DMA,
            pltpu.SemaphoreType.DMA,
        ],
        compiler_params=pltpu.CompilerParams(vmem_limit_bytes=32 * 2**20),
        name="forces",
    )(table, requests, own_codes, fetched, old_force)


def in_hbm(array):
    return pltpu.with_memory_space_constraint(array, pltpu.HBM)


def per_device(field_phase, field_mass, old_force, target_slot, target_star):
    table, requests, own_codes, fetched = gather_table(
        in_hbm(field_phase), in_hbm(field_mass.reshape(1, STAR_DEV)), in_hbm(target_slot.T), in_hbm(target_star.T)
    )
    return forces(table.reshape(OWNERS * 32, 128), requests, own_codes, fetched, in_hbm(old_force))


def solution(mesh):
    split = P(None, ("grp", "blk"))
    return jax.shard_map(
        per_device,
        mesh=mesh,
        in_specs=(split, P(("grp", "blk")), split, split, split),
        out_specs=(split, split, split),
        check_vma=False,
    )
```

```python
import functools

import jax
import jax.numpy as jnp
from jax import lax
from jax.experimental import pallas as pl
from jax.experimental.pallas import tpu as pltpu
from jax.sharding import PartitionSpec as P

MESH = pl.DeviceIdType.MESH
NT = (((1,), (1,)), ((), ()))
F32 = jnp.float32
BF16 = jnp.bfloat16

SOFTEN = 0.01
STEP = 0.5
NZ, NX, NY = 8, 4, 4
STAR_DEV = 512
ACT_DEV = 64
NBR = 100
MOST = 52
OWNERS = 256
STARS = OWNERS * STAR_DEV
PAIRS = OWNERS // 2
UNROLL = 64
ON_MATRIX = tuple(range(0, 64, 4))
STRAIGHT = 3


def table_place(owner):
    core = owner & 1
    x = ((owner >> 1) & 1) * 2 + ((owner >> 4) & 1)
    y = (owner >> 2) & 3
    z = owner >> 5
    ab = jnp.where(core == 1, y * 4 + x, x * 4 + y)
    return core * 128 + ab * 8 + z


def build_requests(slot_ref, star_ref, req_ref, own_ref, place_scr, code_scr, column_scr):
    lane = lax.broadcasted_iota(jnp.int32, (ACT_DEV, 128), 1)
    active = lax.broadcasted_iota(jnp.int32, (ACT_DEV, 128), 0)
    place_scr[...] = jnp.zeros_like(place_scr)
    code_scr[...] = jnp.zeros_like(code_scr)
    place_scr[:, 0:NBR + 1] = slot_ref[...]
    code_scr[:, 0:NBR + 1] = star_ref[...]
    slot = place_scr[...]
    star = code_scr[...]
    owner = (slot * 20165) >> 20
    within = slot - owner * MOST
    place = table_place(owner)
    place_scr[...] = jnp.where((lane > 0) & (lane <= NBR), place >> 1, -1)
    column_scr[...] = within + 64 * (place & 1)
    code_scr[...] = star + active * 512
    own_ref[...] = place * 512 + star

    iota128 = lax.broadcasted_iota(jnp.int32, (128, 128), 0)
    req_ref[...] = jnp.zeros_like(req_ref)

    def add_requests(r, carry):
        rows_a, rows_b = [], []
        for k in range(8):
            line = 8 * r + k
            place_row = place_scr[pl.ds(line, 1), :]
            column_row = column_scr[pl.ds(line, 1), :]
            code_row = code_scr[pl.ds(line, 1), :]
            first = ((code_row & 127) + 128).astype(F32)
            second = (code_row >> 7).astype(F32)
            rows_a.append(jnp.where(iota128 == place_row, 1.0, 0.0).astype(BF16))
            hit = iota128 == column_row
            rows_b.append(
                jnp.concatenate([jnp.where(hit, first, 0.0), jnp.where(hit, second, 0.0)], axis=0).astype(BF16)
            )
        placed = lax.dot_general(
            jnp.concatenate(rows_a, axis=1), jnp.concatenate(rows_b, axis=1), NT, preferred_element_type=F32
        )
        req_ref[0] += placed[:, 0:128]
        req_ref[1] += placed[:, 128:256]
        return carry

    lax.fori_loop(0, ACT_DEV // 8, add_requests, 0)


def gather_kernel(
    phase_hbm, mass_hbm, slot_hbm, star_hbm, out_ref, req_ref, own_ref, fetched,
    phase_ref, mass_ref, slot_ref, star_ref, place_scr, code_scr, column_scr,
    in_sem, z_send, z_recv, a_send, a_recv, b_send, b_recv, c_send, c_recv,
):
    loads = [
        pltpu.make_async_copy(source, target, in_sem.at[n])
        for n, (source, target) in enumerate(
            ((phase_hbm, phase_ref), (mass_hbm, mass_ref), (slot_hbm, slot_ref), (star_hbm, star_ref))
        )
    ]
    for load in loads:
        load.start()
    grp = lax.axis_index("grp")
    blk = lax.axis_index("blk")
    z = grp // 8
    x_lo = (grp // 4) % 2
    y = grp % 4
    x = (blk // 2) * 2 + x_lo
    core = blk % 2
    a = core * x + (1 - core) * y
    b = core * y + (1 - core) * x

    def device(cz, ca, cb, cc):
        cx = core * ca + (1 - core) * cb
        cy = core * cb + (1 - core) * ca
        return (cz * 8 + (cx % 2) * 4 + cy, (cx // 2) * 2 + cc)

    a_up, a_down = (a + 1) % 4, (a + 3) % 4
    b_up, b_down = (b + 1) % 4, (b + 3) % 4
    partners = [device((z + k) % NZ, a, b, core) for k in range(1, NZ)]
    partners += [device(z, a_up, b, core), device(z, a_down, b, core)]
    partners += [device(z, a, b_up, core), device(z, a, b_down, core)]
    partners += [device(z, a, b, 1 - core), device(z, (a + 2) % 4, b, core)]
    if STRAIGHT < 4:
        partners += [device(z, a, (b + 2) % 4, core)]

    barrier = pltpu.get_barrier_semaphore()
    for partner in partners:
        pl.semaphore_signal(barrier, inc=1, device_id=partner, device_id_type=MESH)

    loads[0].wait()
    loads[1].wait()

    for t in range(4):
        lanes = slice(t * 128, t * 128 + 128)
        out_ref[core, b, a, z, t, 0:6, :] = phase_ref[:, lanes]
        out_ref[core, b, a, z, t, 6:7, :] = mass_ref[:, lanes]
        out_ref[core, b, a, z, t, 7:8, :] = jnp.ones((1, 128), F32)

    pl.semaphore_wait(barrier, len(partners))

    started = []
    late = []

    def send(part, send_sem, recv_sem, target):
        copy = pltpu.make_async_remote_copy(
            src_ref=part, dst_ref=part, send_sem=send_sem, recv_sem=recv_sem, device_id=target, device_id_type=MESH
        )
        copy.start()
        started.append(copy)

    def await_recv(part, send_sem, recv_sem):
        while late:
            fetch(*late.pop())
        pltpu.make_async_remote_copy(
            src_ref=part, dst_ref=part, send_sem=send_sem, recv_sem=recv_sem,
            device_id=partners[11], device_id_type=MESH,
        ).wait_recv()

    def block(bb, aa):
        return out_ref.at[core, bb, aa, :, :, pl.ds(0, 7)]

    def part(bb, aa, half):
        return out_ref.at[core, bb, aa, pl.ds(4 * half, 4), :, pl.ds(0, 7)]

    lane8 = lax.broadcasted_iota(jnp.int32, (8, 128), 1)

    def fetch(cc, bb, aa):
        def one_pair(k, carry):
            pair = cc * 64 + (bb * 4 + aa) * 4 + k
            first = jnp.broadcast_to(req_ref[0, pl.ds(pair, 1), :], (8, 128)).astype(jnp.int32)
            second = jnp.broadcast_to(req_ref[1, pl.ds(pair, 1), :], (8, 128)).astype(jnp.int32)
            index = first & 127
            quarter = second & 3
            both = []
            for h in range(2):
                got = None
                for t in range(4):
                    column = jnp.take_along_axis(out_ref[cc, bb, aa, 2 * k + h, t], index, axis=1)
                    got = column if t == 0 else jnp.where(quarter == t, column, got)
                both.append(got)
            fetched[pl.ds(pl.multiple_of(pair * 8, 8), 8), :] = jnp.where(lane8 < 64, both[0], both[1])
            return carry

        lax.fori_loop(0, 4, one_pair, 0, unroll=True)

    for k in range(1, NZ):
        send(out_ref.at[core, b, a, z, :, pl.ds(0, 7)], z_send.at[k], z_recv.at[k], partners[k - 1])
    for k in range(1, NZ):
        await_recv(out_ref.at[core, b, a, (z + NZ - k) % NZ, :, pl.ds(0, 7)], z_send.at[k], z_recv.at[k])

    to_a_up, to_a_down = partners[7], partners[8]
    to_b_up, to_b_down = partners[9], partners[10]
    other = partners[11]

    def send_core(bb, aa, n):
        send(block(bb, aa), c_send.at[n], c_recv.at[n], other)
        late.append((core, bb, aa))

    def send_b(aa, n):
        send(block(b, aa), b_send.at[n, 0], b_recv.at[n, 0], to_b_up)
        send(block(b, aa), b_send.at[n, 1], b_recv.at[n, 1], to_b_down)
        if n >= STRAIGHT:
            send(block(b, aa), b_send.at[n, 2], b_recv.at[n, 2], partners[13])

    def near_b(aa, n):
        await_recv(block(b_down, aa), b_send.at[n, 0], b_recv.at[n, 0])
        if n < STRAIGHT:
            send(part(b_down, aa, 0), b_send.at[n, 2], b_recv.at[n, 2], to_b_up)
        send_core(b_down, aa, 4 * n + 1)
        await_recv(block(b_up, aa), b_send.at[n, 1], b_recv.at[n, 1])
        if n < STRAIGHT:
            send(part(b_up, aa, 1), b_send.at[n, 3], b_recv.at[n, 3], to_b_down)
        send_core(b_up, aa, 4 * n + 2)

    def far_b(aa, n):
        far = (b + 2) % 4
        if n < STRAIGHT:
            await_recv(part(far, aa, 0), b_send.at[n, 2], b_recv.at[n, 2])
            await_recv(part(far, aa, 1), b_send.at[n, 3], b_recv.at[n, 3])
        else:
            await_recv(block(far, aa), b_send.at[n, 2], b_recv.at[n, 2])
        send_core(far, aa, 4 * n + 3)

    send(block(b, a), a_send.at[0], a_recv.at[0], to_a_up)
    send(block(b, a), a_send.at[1], a_recv.at[1], to_a_down)
    send(block(b, a), a_send.at[2], a_recv.at[2], partners[12])
    send_b(a, 0)
    send_core(b, a, 0)
    loads[2].wait()
    loads[3].wait()
    build_requests(slot_ref, star_ref, req_ref, own_ref, place_scr, code_scr, column_scr)

    await_recv(block(b, a_down), a_send.at[0], a_recv.at[0])
    send_b(a_down, 1)
    await_recv(block(b, a_up), a_send.at[1], a_recv.at[1])
    send_b(a_up, 2)
    send_core(b, a_down, 4)
    send_core(b, a_up, 8)
    a_far = (a + 2) % 4
    near_b(a, 0)
    await_recv(block(b, a_far), a_send.at[2], a_recv.at[2])
    send_b(a_far, 3)
    send_core(b, a_far, 12)
    near_b(a_down, 1)
    far_b(a, 0)
    near_b(a_up, 2)
    far_b(a_down, 1)
    near_b(a_far, 3)
    far_b(a_up, 2)
    far_b(a_far, 3)

    oa, ob = b, a
    for n, da in enumerate((0, 3, 1, 2)):
        for m, db in enumerate((0, 3, 1, 2)):
            bb, aa = (ob + db) % 4, (oa + da) % 4
            await_recv(out_ref.at[1 - core, bb, aa, :, :, pl.ds(0, 7)], c_send.at[4 * n + m], c_recv.at[4 * n + m])
            fetch(1 - core, bb, aa)
    for copy in started:
        copy.wait_send()


def gather_table(phase, mass, target_slot, target_star):
    hbm = pl.BlockSpec(memory_space=pltpu.HBM)
    vmem = pl.BlockSpec(memory_space=pltpu.VMEM)
    return pl.pallas_call(
        gather_kernel,
        out_shape=(
            jax.ShapeDtypeStruct((2, 4, 4, NZ, 4, 8, 128), F32),
            jax.ShapeDtypeStruct((2, PAIRS, 128), F32),
            jax.ShapeDtypeStruct((ACT_DEV, 128), jnp.int32),
            jax.ShapeDtypeStruct((PAIRS * 8, 128), F32),
        ),
        in_specs=[hbm] * 4,
        out_specs=(vmem,) * 4,
        scratch_shapes=[
            pltpu.VMEM((6, STAR_DEV), F32),
            pltpu.VMEM((1, STAR_DEV), F32),
            pltpu.VMEM((ACT_DEV, NBR + 1), jnp.int32),
            pltpu.VMEM((ACT_DEV, NBR + 1), jnp.int32),
            pltpu.VMEM((ACT_DEV, 128), jnp.int32),
            pltpu.VMEM((ACT_DEV, 128), jnp.int32),
            pltpu.VMEM((ACT_DEV, 128), jnp.int32),
            pltpu.SemaphoreType.DMA((4,)),
            pltpu.SemaphoreType.DMA((8,)),
            pltpu.SemaphoreType.DMA((8,)),
            pltpu.SemaphoreType.DMA((4,)),
            pltpu.SemaphoreType.DMA((4,)),
            pltpu.SemaphoreType.DMA((4, 4)),
            pltpu.SemaphoreType.DMA((4, 4)),
            pltpu.SemaphoreType.DMA((16,)),
            pltpu.SemaphoreType.DMA((16,)),
        ],
        compiler_params=pltpu.CompilerParams(
            collective_id=0, has_side_effects=True, vmem_limit_bytes=24 * 2**20
        ),
        name="gather_table",
    )(phase, mass, target_slot, target_star)


def split2(v):
    high = v.astype(BF16)
    return high, (v - high.astype(F32)).astype(BF16)


def split3_rows(v):
    high = v.astype(BF16).astype(F32)
    rest = v - high
    middle = rest.astype(BF16).astype(F32)
    return jnp.concatenate([high, middle, rest - middle], axis=0).astype(BF16)


def force_kernel(
    table_ref, req_ref, own_vec, fetched, old_hbm, reg_ref, irr_ref, new_ref,
    own_smem, old_scr, terms, moved, left_scr, own_b, acc, copy_sem, old_sem,
):
    load = pltpu.make_async_copy(old_hbm, old_scr, old_sem)
    load.start()
    fill = pltpu.make_async_copy(own_vec, own_smem, copy_sem)
    fill.start()
    fill.wait()
    lane8 = lax.broadcasted_iota(jnp.int32, (8, 128), 1)
    own = jnp.zeros((8, 128), F32)
    for i in range(ACT_DEV):
        code = own_smem[i, 0]
        tile = table_ref[pl.ds(pl.multiple_of((code >> 7) * 8, 8), 8), :]
        turned = pltpu.roll(tile, (i + 128 - (code & 127)) & 127, 1)
        own = jnp.where(lane8 == i, turned, own)
    own_columns = jnp.transpose(own)
    for c in range(6):
        own_b[c] = jnp.broadcast_to(own_columns[0:ACT_DEV, c:c + 1], (ACT_DEV, 128))

    def neighbour_terms(g):
        base = pl.multiple_of(g * 64, 64)
        lines = pl.ds(pl.multiple_of(g * 8, 8), 8)
        first = req_ref[0, lines, :]
        index = req_ref[1, lines, :].astype(jnp.int32) >> 2
        star_rows = [fetched[pl.ds(base + c, 8, stride=8), :] for c in range(7)]
        own_rows = [
            jnp.take_along_axis(jnp.broadcast_to(own[c:c + 1, :], (8, 128)), index, axis=1) for c in range(6)
        ]
        d = [star_rows[c] - own_rows[c] for c in range(3)]
        w = [star_rows[c] - own_rows[c] for c in range(3, 6)]
        q = SOFTEN + (d[0] * d[0] + d[1] * d[1] + d[2] * d[2])
        dw = d[0] * w[0] + d[1] * w[1] + d[2] * w[2]
        inverse = lax.rsqrt(q)
        square = inverse * inverse
        weight = jnp.where(first > 0.5, star_rows[6] * inverse * square, 0.0)
        radial = 3.0 * dw * square
        for c in range(3):
            terms[pl.ds(base + c, 8, stride=8), :] = weight * d[c]
            terms[pl.ds(base + 3 + c, 8, stride=8), :] = weight * (w[c] - radial * d[c])
        terms[pl.ds(base + 6, 8, stride=8), :] = jnp.zeros((8, 128), F32)
        terms[pl.ds(base + 7, 8, stride=8), :] = jnp.zeros((8, 128), F32)

    iota64 = lax.broadcasted_iota(jnp.int32, (ACT_DEV, 128), 0)

    def add_terms(p, carry):
        lefts, rights = [], []
        for k in range(8):
            pair = 8 * p + k
            t = terms[pl.ds(pl.multiple_of(pair * 8, 8), 8), :]
            high = t.astype(BF16).astype(F32)
            lefts.append(jnp.concatenate([high, t - high], axis=0).astype(BF16))
            index = req_ref[1, pl.ds(pair, 1), :].astype(jnp.int32) >> 2
            rights.append(jnp.where(iota64 == index, 1.0, 0.0).astype(BF16))
        return carry + lax.dot_general(
            jnp.concatenate(lefts, axis=1), jnp.concatenate(rights, axis=1), NT, preferred_element_type=F32
        )

    centre = jnp.sum(own[:, 0:ACT_DEV], axis=1, keepdims=True) * (1.0 / ACT_DEV)
    home = own - centre
    for c in range(6):
        own_b[c] = own_b[c] - jnp.broadcast_to(centre[c:c + 1, :], (ACT_DEV, 128))

    def shift(g, carry):
        base = pl.multiple_of(g * 64, 64)
        rows = [table_ref[pl.ds(base + c, 8, stride=8), :] - centre[c:c + 1, :] for c in range(6)]
        for c in range(6):
            moved[pl.ds(base + c, 8, stride=8), :] = rows[c]
        moved[pl.ds(base + 6, 8, stride=8), :] = rows[0] * rows[3] + rows[1] * rows[4] + rows[2] * rows[5]
        moved[pl.ds(base + 7, 8, stride=8), :] = jnp.ones((8, 128), F32)
        return carry

    lax.fori_loop(0, OWNERS // 2, shift, 0, unroll=2)
    s_own = jnp.sum(home[0:3, :] * home[3:6, :], axis=0, keepdims=True)
    left = jnp.concatenate([-home[3:6, :], -home[0:3, :], jnp.ones((1, 128), F32), s_own], axis=0)
    left_h = left.astype(BF16).astype(F32)
    left_m = (left - left_h).astype(BF16).astype(F32)
    left_l = left - left_h - left_m
    left = jnp.concatenate([left_h, left_h, left_m, left_m, left_h, left_l, jnp.zeros((80, 128), F32)], axis=0)
    left = jnp.transpose(left)[0:ACT_DEV, 0:64]
    none = jnp.zeros((ACT_DEV, 64), F32)
    for n in range(4):
        line = jnp.concatenate([left if k == n else none for k in range(4)], axis=1)
        left_scr[n * 64:n * 64 + 64, :] = line.astype(BF16)
    blank = jnp.zeros((16, 256), BF16)

    acc[...] = jnp.zeros_like(acc)

    def add_shards(g, sums):
        for k in range(UNROLL // 16):
            neighbour_terms(g * (UNROLL // 16) + k)
            sums = add_terms(g * (UNROLL // 16) + k, sums)
        wholes, products = [], []
        for u in range(UNROLL):
            tiles = [pl.multiple_of((g * UNROLL + u) * 32 + 8 * t, 8) for t in range(4)]
            wholes.append(jnp.concatenate([moved[pl.ds(tile, 8), :] for tile in tiles], axis=1))
            products.append(None)
        for first in ON_MATRIX:
            stack = []
            for u in (first, first + 1):
                high = wholes[u].astype(BF16).astype(F32)
                rest = wholes[u] - high
                middle = rest.astype(BF16).astype(F32)
                pair = jnp.concatenate([high, middle], axis=0).astype(BF16)
                last = jnp.concatenate([rest - middle, high], axis=0).astype(BF16)
                for lanes in (slice(0, 256), slice(256, 512)):
                    stack += [pair[:, lanes], pair[:, lanes], last[:, lanes], blank]
            product = jnp.dot(left_scr[...], jnp.concatenate(stack, axis=0), preferred_element_type=F32)
            for k in range(2):
                products[first + k] = jnp.concatenate(
                    [product[128 * k:128 * k + 64], product[128 * k + 64:128 * k + 128]], axis=1
                )
        on = [first + k for first in ON_MATRIX for k in range(2)]
        for u in [u for u in range(UNROLL) if u not in on] + on:
            shard = g * UNROLL + u
            base = pl.multiple_of(shard * 32, 32)
            tiles = [pl.multiple_of(base + 8 * t, 8) for t in range(4)]
            whole = wholes[u]
            mass = jnp.concatenate([table_ref[pl.ds(tile + 6, 1), :] for tile in tiles], axis=1)
            emit = split3_rows(whole * mass)
            quarters = []
            for t in range(4):
                d = [moved[pl.ds(tiles[t] + c, 1), :] - own_b[c] for c in range(3)]
                if products[u] is None:
                    w = [moved[pl.ds(tiles[t] + c, 1), :] - own_b[c] for c in range(3, 6)]
                    dw = d[0] * w[0] + d[1] * w[1] + d[2] * w[2]
                else:
                    dw = products[u][:, t * 128:t * 128 + 128]
                q = (d[0] * d[0] + d[1] * d[1]) + (d[2] * d[2] + SOFTEN)
                inverse = lax.rsqrt(q)
                square = inverse * inverse
                v = square * inverse
                u_ = dw * (v * square)
                quarters.append(split2(v) + split2(u_))
            weights = jnp.concatenate(
                [jnp.concatenate([part[k] for part in quarters], axis=1) for k in range(4)], axis=0
            )
            acc[...] += lax.dot_general(emit, weights, NT, preferred_element_type=F32)
        return sums

    sums = lax.fori_loop(0, OWNERS // UNROLL, add_shards, jnp.zeros((16, ACT_DEV), F32))
    irregular = (sums[0:6, :] + sums[8:14, :]) / NBR
    total = acc[...]
    total = total[0:8] + total[8:16] + total[16:24]
    v_rows = total[:, 0:64] + total[:, 64:128]
    u_rows = total[:, 128:192] + total[:, 192:256]
    home = home[:, 0:ACT_DEV]
    v_terms = v_rows - home * v_rows[7:8]
    u_terms = u_rows - home * u_rows[7:8]
    accel = v_terms[0:3] / STARS
    jerk = (v_terms[3:6] - 3.0 * u_terms[0:3]) / STARS

    load.wait()
    old = old_scr[...]
    accel_new = accel + irregular[0:3]
    jerk_new = jerk + irregular[3:6]
    difference = old[0:3] - accel_new
    snap = -6.0 * difference - STEP * (4.0 * old[3:6] + 2.0 * jerk_new)
    crackle = 12.0 * difference + 6.0 * STEP * (old[3:6] + jerk_new)
    reg_ref[0:3, :] = accel
    reg_ref[3:6, :] = jerk
    irr_ref[...] = irregular
    new_ref[0:3, :] = own[0:3, 0:ACT_DEV] + STEP * STEP / 24.0 * snap + STEP * STEP / 120.0 * crackle
    new_ref[3:6, :] = own[3:6, 0:ACT_DEV] + STEP / 6.0 * snap + STEP / 24.0 * crackle


def forces(table, requests, own_codes, fetched, old_force):
    vmem = pl.BlockSpec(memory_space=pltpu.VMEM)
    out = jax.ShapeDtypeStruct((6, ACT_DEV), F32)
    return pl.pallas_call(
        force_kernel,
        out_shape=(out, out, out),
        in_specs=[vmem] * 4 + [pl.BlockSpec(memory_space=pltpu.HBM)],
        out_specs=(vmem,) * 3,
        scratch_shapes=[
            pltpu.SMEM((ACT_DEV, 128), jnp.int32),
            pltpu.VMEM((6, ACT_DEV), F32),
            pltpu.VMEM((PAIRS * 8, 128), F32),
            pltpu.VMEM((OWNERS * 32, 128), F32),
            pltpu.VMEM((256, 256), BF16),
            pltpu.VMEM((6, ACT_DEV, 128), F32),
            pltpu.VMEM((24, 256), F32),
            pltpu.SemaphoreType.DMA,
            pltpu.SemaphoreType.DMA,
        ],
        compiler_params=pltpu.CompilerParams(vmem_limit_bytes=32 * 2**20),
        name="forces",
    )(table, requests, own_codes, fetched, old_force)


def in_hbm(array):
    return pltpu.with_memory_space_constraint(array, pltpu.HBM)


def per_device(field_phase, field_mass, old_force, target_slot, target_star):
    table, requests, own_codes, fetched = gather_table(
        in_hbm(field_phase), in_hbm(field_mass.reshape(1, STAR_DEV)), in_hbm(target_slot.T), in_hbm(target_star.T)
    )
    return forces(table.reshape(OWNERS * 32, 128), requests, own_codes, fetched, in_hbm(old_force))


def solution(mesh):
    split = P(None, ("grp", "blk"))
    return jax.shard_map(
        per_device,
        mesh=mesh,
        in_specs=(split, P(("grp", "blk")), split, split, split),
        out_specs=(split, split, split),
        check_vma=False,
    )
```
